32 devices in a mesh: slab: 8 (over z, x), elec: 4 (over y, core).
Axes of the slice: x: 2, y: 2, z: 4, core: 2. Of those that a mesh axis runs over, the one named last changes fastest.
Arguments:
- potentials: float32 [128, 16, 128, 128], P('elec', None, 'slab'), may hold values from -6 to 6
- conductivity: float32 [16, 128, 128], P(None, 'slab'), may hold values from 0.1 to 1
- quadrupoles: int32 [512, 4], P('elec'), may hold values from 0 to 127, as said below
Outputs:
- jacobian: bfloat16 [512, 16, 128, 128], P('elec', 'slab')
The draws below stay inside these ranges and needn't reach their ends.
Inputs may be any that keep to these rules, and one draw needn't show every extreme that they name: `quadrupoles`: rows g * 128 to (g + 1) * 128 - 1 are the measurements of group g; electrode e belongs to group e // 32. A and B are two different electrodes of the row's own group; M and N are two different electrodes of other groups. The rows of one group name, in M or N, at most 4 different electrodes of any one other group, and exactly 4 of some other group.
All inputs are finite; a program needn't handle non-finite values.
Results may differ from the reference program's by a relative error of at most 0.0058.
Values may be sent and summed in bfloat16 or wider, within the bound.
A program may use at most 256 MiB of HBM per device.

```python
import math
import jax
import jax.numpy as jnp
from jax import lax

CELLS_ALONG_X = 128
CELLS_ALONG_Y = 128
GROUP_CURRENTS = 32
GROUP_READINGS = 128
REQ = 4
CELLS_ALONG_Z = 16
E = 128
TOTAL_READINGS = 512
N_ELEC = 4


def draw_quadrupoles(key, part):
    block_list = []
    for group_idx in range(N_ELEC):
        group_key = jax.random.fold_in(key, group_idx)
        key_sequence = jax.random.split(group_key, 4 + N_ELEC)
        first_local_index = jax.random.randint(key_sequence[0], (GROUP_READINGS,), 0, GROUP_CURRENTS)
        second_local_index = (first_local_index + jax.random.randint(key_sequence[1], (GROUP_READINGS,), 1, GROUP_CURRENTS)) % GROUP_CURRENTS
        member_list = []
        valid_list = []
        for offset in range(1, N_ELEC):
            other_group = (group_idx + offset) % N_ELEC
            chosen = jax.random.permutation(key_sequence[3 + offset], GROUP_CURRENTS)[:REQ] + other_group * GROUP_CURRENTS
            if offset == 1:
                limit = REQ
            else:
                limit = jax.random.randint(jax.random.fold_in(key_sequence[2], offset), (), 1, REQ + 1)
            member_list.append(chosen)
            valid_list.append(jnp.arange(REQ) < limit)
        members = jnp.concatenate(member_list, 0)
        valid_flags = jnp.concatenate(valid_list, 0)
        ranking = jnp.where(valid_flags, 0, members.shape[0]) + jnp.arange(members.shape[0])
        eligible = members[jnp.argsort(ranking)]
        length_total = jnp.sum(valid_flags.astype(jnp.int32))
        row_index_list = jnp.arange(GROUP_READINGS)
        probe_first = eligible[row_index_list % length_total]
        shift_amount = jax.random.randint(key_sequence[3], (GROUP_READINGS,), 0, length_total - 1)
        probe_second = eligible[(row_index_list + 1 + shift_amount) % length_total]
        block_list.append(jnp.stack([group_idx * GROUP_CURRENTS + first_local_index, group_idx * GROUP_CURRENTS + second_local_index, probe_first, probe_second], 1))
    return jnp.concatenate(block_list, 0).astype(jnp.int32)


def level_of(key, shape, cuts, low, top_value):
    gain, own = 1.0, jax.random.fold_in(key, 6)
    for dim, shards_of in cuts:
        steps = jnp.exp(jax.random.uniform(jax.random.fold_in(own, dim), (shards_of,), jnp.float32, low / len(cuts), top_value / len(cuts)))
        gain = gain * jnp.repeat(steps, shape[dim] // shards_of).reshape([-1 if axis == dim else 1 for axis in range(len(shape))])
    return gain


def bell_draw(own_key, extent, scale, most, pieces=(), kind=jnp.bfloat16):
    result = scale * jax.random.normal(own_key, extent, jnp.float32)
    if pieces:
        result = result * level_of(own_key, extent, pieces, -0.22, 0.18)
    return jnp.clip(result, -most, most).astype(kind)


def setup_inputs(seed: int = 0) -> dict:
    keys = jax.random.split(jax.random.key(seed), 4)
    return {
        "potentials": bell_draw(keys[0], (E, CELLS_ALONG_Z, CELLS_ALONG_X, CELLS_ALONG_Y), 1.0, 6.0, ((0, 4), (2, 8)), jnp.float32),
        "conductivity": jnp.clip(jnp.exp(math.log(1.0) - 2.3025851 * jax.random.uniform(keys[1], (CELLS_ALONG_Z, CELLS_ALONG_X, CELLS_ALONG_Y), jnp.float32) ** level_of(keys[1], (CELLS_ALONG_Z, CELLS_ALONG_X, CELLS_ALONG_Y), ((1, 8),), -0.2, 0.2)), 0.1, 1.0),
        "quadrupoles": draw_quadrupoles(jax.random.fold_in(keys[3], 71), 0),
    }


def gradients(potentials):
    padded = jnp.pad(potentials, ((0, 0), (1, 1), (1, 1), (1, 1)))
    grad_z = (padded[:, 2:, 1:-1, 1:-1] - padded[:, :-2, 1:-1, 1:-1]) * 0.5
    grad_x = (padded[:, 1:-1, 2:, 1:-1] - padded[:, 1:-1, :-2, 1:-1]) * 0.5
    grad_y = (padded[:, 1:-1, 1:-1, 2:] - padded[:, 1:-1, 1:-1, :-2]) * 0.5
    return jnp.stack([grad_z, grad_x, grad_y], 1).astype(jnp.bfloat16)


def reference(potentials, conductivity, quadrupoles):
    grad = gradients(potentials)

    def block_rows(quad_block):
        source_grad = grad[quad_block[:, 0]].astype(jnp.float32) - grad[quad_block[:, 1]].astype(jnp.float32)
        probe_grad = grad[quad_block[:, 2]].astype(jnp.float32) - grad[quad_block[:, 3]].astype(jnp.float32)
        summed = jnp.sum(source_grad * probe_grad, axis=1)
        return (-(conductivity[None] * summed)).astype(jnp.bfloat16)

    number_of_blocks = TOTAL_READINGS // 16
    output_rows = lax.map(block_rows, quadrupoles.reshape(number_of_blocks, 16, 4))
    return output_rows.reshape(TOTAL_READINGS, CELLS_ALONG_Z, CELLS_ALONG_X, CELLS_ALONG_Y)
```

```python
import functools

import jax
import jax.numpy as jnp
from jax import lax
from jax.experimental import pallas as pl
from jax.experimental.pallas import tpu as pltpu
from jax.sharding import PartitionSpec as P

MESH = pl.DeviceIdType.MESH
REQ = 4
PARTS = 4
SPAN = 12.5
LEVELS = 32767.0
COND_MID = 0.55
COND_STEPS = 32766.0 / 0.45


def lists(quadrupoles, per_group, groups):
    me = lax.axis_index("elec")
    ids = jnp.arange(per_group * groups, dtype=jnp.int32)
    owner = ids // per_group
    away = (owner - me) % groups
    named = jnp.any(quadrupoles[:, 2:4].reshape(-1)[:, None] == ids[None, :], axis=0)
    before = (owner[:, None] == owner[None, :]) & (ids[None, :] < ids[:, None])
    rank = jnp.sum((before & named[None, :]).astype(jnp.int32), axis=1)
    other = (away - 1) * REQ + jnp.minimum(rank, REQ - 1)
    slot = jnp.where(away == 0, ids - me * per_group, other)
    index = jnp.sum(jnp.where(quadrupoles[:, :, None] == ids, slot, 0), axis=-1)
    steps = jnp.arange(groups, dtype=jnp.int32)[:, None, None]
    lanes = jnp.arange(128, dtype=jnp.int32)[None, :, None]
    hit = named & (away == steps) & (rank == lanes)
    asked = jnp.sum(jnp.where(hit, ids % per_group, 0), axis=-1)
    return index.astype(jnp.int32), jnp.broadcast_to(asked[:, None, :], (groups, 8, 128))


def minus(first, second):
    return first.astype(jnp.float32) - second.astype(jnp.float32)


def decode(code):
    root = code.astype(jnp.int32).astype(jnp.float32) * (SPAN**0.125 / LEVELS)
    square = root * root
    fourth = square * square
    return (root * jnp.abs(root)) * square * fourth


def encode(step):
    level = jnp.exp2(jnp.log2(jnp.abs(step) * (1.0 / SPAN)) * 0.125) * LEVELS
    level = (level + 0.5).astype(jnp.int32)
    return jnp.where(step < 0, -level, level).astype(jnp.int16)


def exchange_kernel(slabs, groups, *refs):
    pot, cond, asked, index, out = refs[:5]
    pot_v, cond_v, enc, cin, field, cond_code, cond_in = refs[5:12]
    asked_in, asked_s, own, box, result = refs[12:17]
    far = refs[17 : 17 + slabs]
    pot_sem, plane_send, plane_recv, fwd_send, cond_send, cond_recv = refs[17 + slabs : 23 + slabs]
    ask_send, ask_recv, far_send, far_recv, out_sem, local = refs[23 + slabs :]

    count, depth, rows, width = pot.shape
    slots = rows + 1
    half = slabs // 2
    pair = half // 2
    x_size = rows * slabs
    tall = x_size + 16
    readings = out.shape[0]
    me = lax.axis_index("slab")
    group = lax.axis_index("elec")
    upper = me // half
    near0 = upper * half
    far0 = (1 - upper) * half
    inner = (me >= half - pair) & (me < half + pair)
    my_rows = pl.ds(pl.multiple_of(me * rows, rows), rows)

    def pot_copy(d):
        return pltpu.make_async_copy(
            pot.at[:, pl.ds(2 * d, 2)], pot_v.at[:, pl.ds(2 * d, 2)], pot_sem.at[d]
        )

    def dest(n):
        first, second = jnp.where(inner, far0, near0), jnp.where(inner, near0, far0)
        return jnp.where(n < half, first + n, second + n - half)

    @pl.loop(0, slabs)
    def _(n):
        pot_copy(dest(n)).start()

    cond_load = pltpu.make_async_copy(cond, cond_v, local.at[0])
    cond_load.start()

    barrier = pltpu.get_barrier_semaphore()
    for step in range(1, slabs):
        pl.semaphore_signal(barrier, inc=1, device_id={"slab": lax.rem(me + step, slabs)}, device_id_type=MESH)
    for step in range(1, groups):
        pl.semaphore_signal(barrier, inc=1, device_id={"elec": lax.rem(group + step, groups)}, device_id_type=MESH)

    blank = jnp.zeros((slots, count, width), jnp.int16)
    enc[0] = blank
    enc[depth + 1] = blank

    @pl.when(me == 0)
    def _():
        @pl.loop(1, slabs)
        def _(r):
            cin[r, 0] = blank

    @pl.when(me == slabs - 1)
    def _():
        @pl.loop(0, slabs - 1)
        def _(r):
            cin[r, 3] = blank

    @pl.loop(0, 2 * count)
    def _(k):
        base = (count + k) * tall
        edge = jnp.zeros((8, width), jnp.float32)
        field[pl.ds(pl.multiple_of(base, 8), 8), :] = edge
        field[pl.ds(pl.multiple_of(base + tall - 8, 8), 8), :] = edge

    pl.semaphore_wait(barrier, slabs + groups - 2)

    def ask_copy(step):
        return pltpu.make_async_remote_copy(
            src_ref=asked.at[step],
            dst_ref=asked_in.at[step],
            send_sem=ask_send.at[step],
            recv_sem=ask_recv.at[step],
            device_id={"elec": lax.rem(group + step, groups)},
            device_id_type=MESH,
        )

    for step in range(1, groups):
        ask_copy(step).start()

    def plane_copy(slot, d):
        return pltpu.make_async_remote_copy(
            src_ref=enc.at[2 * d + slot],
            dst_ref=cin.at[me, slot],
            send_sem=plane_send.at[slot, d],
            recv_sem=plane_recv.at[slot, me],
            device_id={"slab": d},
            device_id_type=MESH,
        )

    def plane_wait(slot, r):
        pltpu.make_async_remote_copy(
            src_ref=enc.at[slot],
            dst_ref=cin.at[r, slot],
            send_sem=plane_send.at[slot, r],
            recv_sem=plane_recv.at[slot, r],
            device_id={"slab": r},
            device_id_type=MESH,
        ).wait_recv()

    def forward_up(r):
        return pltpu.make_async_remote_copy(
            src_ref=cin.at[r, 2],
            dst_ref=cin.at[r, 0],
            send_sem=fwd_send.at[0, r],
            recv_sem=plane_recv.at[0, r],
            device_id={"slab": lax.rem(me + 1, slabs)},
            device_id_type=MESH,
        )

    def forward_down(r):
        return pltpu.make_async_remote_copy(
            src_ref=cin.at[r, 1],
            dst_ref=cin.at[r, 3],
            send_sem=fwd_send.at[1, r],
            recv_sem=plane_recv.at[3, r],
            device_id={"slab": lax.rem(me + slabs - 1, slabs)},
            device_id_type=MESH,
        )

    ups = (me != slabs - 1) & (me != half - 1)
    downs = (me != 0) & (me != half)

    def cond_copy(step):
        to = lax.rem(me + step, slabs)
        return pltpu.make_async_remote_copy(
            src_ref=cond_code.at[pl.ds(to * 2, 2)],
            dst_ref=cond_in.at[:, my_rows, :],
            send_sem=cond_send.at[step],
            recv_sem=cond_recv.at[step],
            device_id={"slab": to},
            device_id_type=MESH,
        )

    own_cond = pltpu.make_async_copy(cond_code.at[pl.ds(me * 2, 2)], cond_in.at[:, my_rows, :], local.at[1])
    own_planes = pltpu.make_async_copy(enc.at[pl.ds(2 * me, 4)], cin.at[me], local.at[2])

    cond_load.wait()

    @pl.loop(0, depth)
    def _(z):
        level = (cond_v[z] - COND_MID) * COND_STEPS
        level = level + jnp.where(level < 0, -0.5, 0.5)
        cond_code[z] = level.astype(jnp.int32).astype(jnp.int16)

    for step in range(1, slabs):
        cond_copy(step).start()
    own_cond.start()

    def encode_plane(z):
        reached = jnp.zeros((count, width), jnp.float32)
        for slot in range(slots):
            start = z * rows + max(slot - 1, 0)
            wanted = pot_v.reshape(count * depth * rows, width)[pl.ds(start, count, stride=depth * rows), :]
            code = encode(wanted - reached)
            enc[z + 1, slot] = code
            reached = reached + decode(code)

    @pl.loop(0, 2 * slabs)
    def _(n):
        part, place = n // half, lax.rem(n, half)
        i = lax.rem(part, 2)
        d = dest((part // 2) * half + place)

        @pl.when(i == 0)
        def _():
            pot_copy(d).wait()

        encode_plane(2 * d + i)
        close = d // half == upper

        @pl.when((d != me) & (close | inner))
        def _():
            plane_copy(1 + i, d).start()

    own_planes.start()

    def edge_copies(d, act):
        close = d // half == upper

        @pl.when((d > 0) & (close | (d == half)))
        def _():
            act(plane_copy(0, d))

        @pl.when((d < slabs - 1) & (close | (d == half - 1)))
        def _():
            act(plane_copy(3, d))

    @pl.when(inner)
    def _():
        edge_copies(jnp.where(upper == 0, half, half - 1), lambda copy: copy.start())

    @pl.loop(0, half)
    def _(j):
        d = near0 + j

        @pl.when(d != me)
        def _():
            edge_copies(d, lambda copy: copy.start())

    for step in range(1, groups):
        ask_copy(step).wait()
    to_scalar = pltpu.make_async_copy(asked_in, asked_s, local.at[3])
    to_scalar.start()
    to_scalar.wait()
    for step in range(1, slabs):
        cond_copy(step).wait_recv()
    own_cond.wait()

    def decode_plane(r, slot):
        reached = jnp.zeros((count, width), jnp.float32)
        for k in range(slots):
            reached = reached + decode(cin[r, slot, k])
            if k > 0:
                field[pl.ds(slot * count * tall + 8 + r * rows + k - 1, count, stride=tall), :] = reached

    row_lane = lax.broadcasted_iota(jnp.int32, (rows, width), 1)

    def gradients(b):
        @pl.loop(0, count)
        def _(e):
            for i in range(2):
                def at(slot, shift):
                    return field[pl.ds((slot * count + e) * tall + 8 + b * rows + shift, rows), :]

                here = at(1 + i, 0)
                right = jnp.where(row_lane < width - 1, pltpu.roll(here, width - 1, 1), 0.0)
                left = jnp.where(row_lane > 0, pltpu.roll(here, 1, 1), 0.0)
                own[b, e, 0, i] = ((at(2 + i, 0) - at(i, 0)) * 0.5).astype(jnp.bfloat16)
                own[b, e, 1, i] = ((at(1 + i, 1) - at(1 + i, -1)) * 0.5).astype(jnp.bfloat16)
                own[b, e, 2, i] = ((right - left) * 0.5).astype(jnp.bfloat16)

    def far_copy(k, step):
        return pltpu.make_async_remote_copy(
            src_ref=box.at[k, step - 1],
            dst_ref=far[k].at[pl.ds((groups - 1 - step) * REQ, REQ)],
            send_sem=far_send.at[k, step],
            recv_sem=far_recv.at[k, step],
            device_id={"elec": lax.rem(group + step, groups)},
            device_id_type=MESH,
        )

    def offer(k, b):
        gradients(b)
        for step in range(1, groups):
            for which in range(REQ):
                chosen = asked_s[groups - step, 0, which]
                box[k, step - 1, which] = own[b, chosen]
            far_copy(k, step).start()

    def result_copy(b):
        return pltpu.make_async_copy(
            result.at[b], out.at[:, :, pl.ds(pl.multiple_of(b * rows, rows), rows), :], out_sem.at[b]
        )

    def finish(k, b):
        for step in range(1, groups):
            far_copy(k, step).wait_recv()
        for i in range(2):
            weight = cond_in[i, pl.ds(pl.multiple_of(b * rows, rows), rows), :]
            weight = -(weight.astype(jnp.int32).astype(jnp.float32) * (1.0 / COND_STEPS) + COND_MID)

            @pl.loop(0, readings // 4)
            def _(block, i=i, weight=weight):
                for n in range(4):
                    m = block * 4 + n
                    first, second, third, fourth = index[4 * m], index[4 * m + 1], index[4 * m + 2], index[4 * m + 3]
                    total = None
                    for way in range(3):
                        source = minus(own[b, first, way, i], own[b, second, way, i])
                        probe = minus(far[k][third, way, i], far[k][fourth, way, i])
                        total = source * probe if total is None else total + source * probe
                    result[b, m, i] = (weight * total).astype(jnp.bfloat16)

        result_copy(b).start()

    @pl.loop(0, half)
    def _(j):
        r = near0 + j

        @pl.when(r == me)
        def _():
            own_planes.wait()

        @pl.when(r != me)
        def _():
            plane_wait(1, r)
            plane_wait(2, r)

            @pl.when(me > 0)
            def _():
                plane_wait(0, r)

            @pl.when(me < slabs - 1)
            def _():
                plane_wait(3, r)

        @pl.loop(0, 4)
        def _(slot):
            decode_plane(r, slot)

    first = upper * (half + 1)

    for j in range(half - 1):
        offer(j, first + j)
    for j in range(half - 1):
        finish(j, first + j)

    def take(r0):
        @pl.loop(0, pair)
        def _(j):
            plane_wait(1, r0 + j)

            @pl.when(downs)
            def _():
                forward_down(r0 + j).start()

            decode_plane(r0 + j, 1)

        @pl.loop(0, pair)
        def _(j):
            plane_wait(2, r0 + j)

            @pl.when(ups)
            def _():
                forward_up(r0 + j).start()

            decode_plane(r0 + j, 2)

    def take_edges(r0):
        @pl.loop(0, pair)
        def _(j):
            @pl.when(me > 0)
            def _():
                plane_wait(0, r0 + j)

            decode_plane(r0 + j, 0)

            @pl.when(me < slabs - 1)
            def _():
                plane_wait(3, r0 + j)

            decode_plane(r0 + j, 3)

    take(far0 + (1 - upper) * 0 + upper * pair)

    @pl.when(jnp.logical_not(inner))
    def _():
        for i in range(2):
            @pl.loop(0, half)
            def _(j, i=i):
                plane_copy(1 + i, far0 + j).start()

        edge_copies(jnp.where(upper == 0, half, half - 1), lambda copy: copy.start())

    take_edges(far0 + upper * pair)
    for j in range(half - 1, half + 1):
        offer(j, j)
    for j in range(half - 1, half + 1):
        finish(j, j)

    take(far0 + (1 - upper) * pair)
    take_edges(far0 + (1 - upper) * pair)
    last = (1 - upper) * (half + 1)

    for j in range(half - 1):
        offer(half + 1 + j, last + j)
    for j in range(half - 1):
        finish(half + 1 + j, last + j)

    @pl.loop(0, slabs)
    def _(d):
        result_copy(d).wait()

        @pl.when(d != me)
        def _():
            plane_copy(1, d).wait_send()
            plane_copy(2, d).wait_send()
            edge_copies(d, lambda copy: copy.wait_send())

        @pl.when(d // half != upper)
        def _():
            @pl.when(ups)
            def _():
                forward_up(d).wait_send()

            @pl.when(downs)
            def _():
                forward_down(d).wait_send()

    for step in range(1, slabs):
        cond_copy(step).wait_send()
    for k in range(slabs):
        for step in range(1, groups):
            far_copy(k, step).wait_send()


def exchange(potentials, conductivity, asked, index, slabs, groups):
    count, depth, rows, width = potentials.shape
    readings = index.shape[0]
    x_size = rows * slabs
    anywhere = pl.BlockSpec(memory_space=pl.ANY)
    dma = pltpu.SemaphoreType.DMA
    bf16, f32, i16 = jnp.bfloat16, jnp.float32, jnp.int16
    asks = (groups - 1) * REQ
    return pl.pallas_call(
        functools.partial(exchange_kernel, slabs, groups),
        out_shape=jax.ShapeDtypeStruct((readings, 2, x_size, width), bf16),
        in_specs=[anywhere, anywhere, pl.BlockSpec(memory_space=pltpu.VMEM), pl.BlockSpec(memory_space=pltpu.SMEM)],
        out_specs=anywhere,
        scratch_shapes=[
            pltpu.VMEM((count, depth, rows, width), f32),
            pltpu.VMEM((depth, rows, width), f32),
            pltpu.VMEM((depth + 2, rows + 1, count, width), i16),
            pltpu.VMEM((slabs, 4, rows + 1, count, width), i16),
            pltpu.VMEM((4 * count * (x_size + 16), width), f32),
            pltpu.VMEM((depth, rows, width), i16),
            pltpu.VMEM((2, x_size, width), i16),
            pltpu.VMEM((groups, 8, 128), jnp.int32),
            pltpu.SMEM((groups, 8, 128), jnp.int32),
            pltpu.VMEM((slabs, count, 3, 2, rows, width), bf16),
            pltpu.VMEM((slabs, groups - 1, REQ, 3, 2, rows, width), bf16),
            pltpu.VMEM((slabs, readings, 2, rows, width), bf16),
        ]
        + [pltpu.VMEM((asks, 3, 2, rows, width), bf16)] * slabs
        + [
            dma((slabs,)),
            dma((4, slabs)),
            dma((4, slabs)),
            dma((2, slabs)),
            dma((slabs,)),
            dma((slabs,)),
            dma((groups,)),
            dma((groups,)),
            dma((slabs, groups)),
            dma((slabs, groups)),
            dma((slabs,)),
            dma((4,)),
        ],
        compiler_params=pltpu.CompilerParams(
            collective_id=0, has_side_effects=True, vmem_limit_bytes=50 * 1024 * 1024
        ),
        name="exchange",
    )(potentials, conductivity, asked, index.reshape(-1))


def deliver_kernel(source, target, done):
    share = source.shape[0] // PARTS
    copies = [
        pltpu.make_async_copy(source.at[pl.ds(k * share, share)], target.at[pl.ds(k * share, share)], done.at[k])
        for k in range(PARTS)
    ]
    for copy in copies:
        copy.start()
    for copy in copies:
        copy.wait()


def deliver(rows):
    return pl.pallas_call(
        deliver_kernel,
        out_shape=jax.ShapeDtypeStruct(rows.shape, rows.dtype),
        in_specs=[pl.BlockSpec(memory_space=pl.ANY)],
        out_specs=pl.BlockSpec(memory_space=pl.ANY),
        scratch_shapes=[pltpu.SemaphoreType.DMA((PARTS,))],
        compiler_params=pltpu.CompilerParams(vmem_limit_bytes=1024 * 1024),
        name="deliver",
    )(rows)


def general(potentials, conductivity, quadrupoles):
    shifted = lax.all_to_all(potentials, "slab", split_axis=1, concat_axis=2, tiled=True)
    cond = lax.all_to_all(conductivity[None], "slab", split_axis=1, concat_axis=2, tiled=True)[0]
    slabs = lax.axis_size("slab")
    ends = slabs - 1
    last = shifted.shape[1] - 1
    below = lax.ppermute(shifted[:, last:], "slab", [(i, i + 1) for i in range(ends)])
    above = lax.ppermute(shifted[:, :1], "slab", [(i + 1, i) for i in range(ends)])
    tall = jnp.concatenate([below, shifted, above], axis=1)
    wide = jnp.pad(shifted, ((0, 0), (0, 0), (1, 1), (1, 1)))
    grads = jnp.stack(
        [
            (tall[:, 2:] - tall[:, :-2]) * 0.5,
            (wide[:, :, 2:, 1:-1] - wide[:, :, :-2, 1:-1]) * 0.5,
            (wide[:, :, 1:-1, 2:] - wide[:, :, 1:-1, :-2]) * 0.5,
        ],
        1,
    ).astype(jnp.bfloat16)
    table = lax.all_gather(grads.reshape(grads.shape[0], 3, -1), "elec", axis=0, tiled=True)
    ids = jnp.arange(table.shape[0], dtype=jnp.int32)
    hot = (quadrupoles[:, :, None] == ids).astype(jnp.bfloat16)
    flat = table.reshape(table.shape[0], -1)
    shape = (quadrupoles.shape[0], 3, -1)
    source = jnp.dot(hot[:, 0] - hot[:, 1], flat, preferred_element_type=jnp.float32).reshape(shape)
    probe = jnp.dot(hot[:, 2] - hot[:, 3], flat, preferred_element_type=jnp.float32).reshape(shape)
    rows = -(cond.reshape(-1)[None] * jnp.sum(source * probe, axis=1))
    return rows.astype(jnp.bfloat16).reshape((quadrupoles.shape[0],) + shifted.shape[1:])


def shards(potentials, conductivity, quadrupoles):
    slabs, groups = lax.axis_size("slab"), lax.axis_size("elec")
    count, depth, rows, width = potentials.shape
    fits = rows == 16 and width == 128 and depth == 2 * slabs and slabs % 4 == 0
    if not fits or count % 16 or quadrupoles.shape[0] % 4:
        return general(potentials, conductivity, quadrupoles)
    index, asked = lists(quadrupoles, count, groups)
    return deliver(exchange(potentials, conductivity, asked, index, slabs, groups))


def solution(mesh):
    in_specs = (P("elec", None, "slab", None), P(None, "slab", None), P("elec", None))
    out_specs = P("elec", "slab", None, None)
    return jax.shard_map(shards, mesh=mesh, in_specs=in_specs, out_specs=out_specs, check_vma=False)
```

```python
import functools

import jax
import jax.numpy as jnp
from jax import lax
from jax.experimental import pallas as pl
from jax.experimental.pallas import tpu as pltpu
from jax.sharding import PartitionSpec as P

MESH = pl.DeviceIdType.MESH
REQ = 4
PARTS = 4
SPAN = 12.5
LEVELS = 32767.0
COND_MID = 0.55
COND_STEPS = 32766.0 / 0.45


def lists(quadrupoles, per_group, groups):
    me = lax.axis_index("elec")
    ids = jnp.arange(per_group * groups, dtype=jnp.int32)
    owner = ids // per_group
    away = (owner - me) % groups
    named = jnp.any(quadrupoles[:, 2:4].reshape(-1)[:, None] == ids[None, :], axis=0)
    before = (owner[:, None] == owner[None, :]) & (ids[None, :] < ids[:, None])
    rank = jnp.sum((before & named[None, :]).astype(jnp.int32), axis=1)
    other = (away - 1) * REQ + jnp.minimum(rank, REQ - 1)
    slot = jnp.where(away == 0, ids - me * per_group, other)
    index = jnp.sum(jnp.where(quadrupoles[:, :, None] == ids, slot, 0), axis=-1)
    steps = jnp.arange(groups, dtype=jnp.int32)[:, None, None]
    lanes = jnp.arange(128, dtype=jnp.int32)[None, :, None]
    hit = named & (away == steps) & (rank == lanes)
    asked = jnp.sum(jnp.where(hit, ids % per_group, 0), axis=-1)
    return index.astype(jnp.int32), jnp.broadcast_to(asked[:, None, :], (groups, 8, 128))


def minus(first, second):
    return first.astype(jnp.float32) - second.astype(jnp.float32)


def decode(code):
    root = code.astype(jnp.int32).astype(jnp.float32) * (SPAN**0.125 / LEVELS)
    square = root * root
    fourth = square * square
    return (root * jnp.abs(root)) * square * fourth


def encode(step):
    level = jnp.exp2(jnp.log2(jnp.abs(step) * (1.0 / SPAN)) * 0.125) * LEVELS
    level = (level + 0.5).astype(jnp.int32)
    return jnp.where(step < 0, -level, level).astype(jnp.int16)


def exchange_kernel(slabs, groups, *refs):
    pot, cond, asked, index, out = refs[:5]
    pot_v, cond_v, stage, enc, cin, field, cond_code, cond_in = refs[5:13]
    asked_in, asked_s, place_v, place_s, own, box = refs[13:19]
    far = refs[19 : 19 + slabs]
    plane_send, plane_recv, fwd_send, cond_send, cond_recv = refs[19 + slabs : 24 + slabs]
    ask_send, ask_recv, far_send, far_recv, pot_sem, local = refs[24 + slabs :]

    count, depth, rows, width = pot.shape
    slots = rows + 1
    some = count // 2
    half = slabs // 2
    x_size = rows * slabs
    tall = x_size + 16
    readings = out.shape[0]
    me = lax.axis_index("slab")
    group = lax.axis_index("elec")
    upper = me // half
    near0 = upper * half
    far0 = (1 - upper) * half
    my_rows = pl.ds(pl.multiple_of(me * rows, rows), rows)

    share = count // PARTS
    loads = [
        pltpu.make_async_copy(pot.at[pl.ds(k * share, share)], pot_v.at[pl.ds(k * share, share)], pot_sem.at[k])
        for k in range(PARTS)
    ]
    cond_load = pltpu.make_async_copy(cond, cond_v, local.at[0])

    barrier = pltpu.get_barrier_semaphore()
    for step in range(1, groups):
        pl.semaphore_signal(barrier, inc=1, device_id={"elec": lax.rem(group + step, groups)}, device_id_type=MESH)
    for step in range(1, slabs):
        pl.semaphore_signal(barrier, inc=1, device_id={"slab": lax.rem(me + step, slabs)}, device_id_type=MESH)
    for copy in loads:
        copy.start()
    cond_load.start()

    blank = jnp.zeros((2, slots, some, width), jnp.int16)
    enc[0] = blank
    enc[depth + 1] = blank

    @pl.when(me == 0)
    def _():
        @pl.loop(1, slabs)
        def _(r):
            cin[r, 0] = blank

    @pl.when(me == slabs - 1)
    def _():
        @pl.loop(0, slabs - 1)
        def _(r):
            cin[r, 3] = blank

    @pl.loop(0, 2 * count)
    def _(k):
        base = (count + k) * tall
        edge = jnp.zeros((8, width), jnp.float32)
        field[pl.ds(pl.multiple_of(base, 8), 8), :] = edge
        field[pl.ds(pl.multiple_of(base + tall - 8, 8), 8), :] = edge

    pl.semaphore_wait(barrier, slabs + groups - 2)

    def ask_copy(step):
        return pltpu.make_async_remote_copy(
            src_ref=asked.at[step],
            dst_ref=asked_in.at[step],
            send_sem=ask_send.at[step],
            recv_sem=ask_recv.at[step],
            device_id={"elec": lax.rem(group + step, groups)},
            device_id_type=MESH,
        )

    for step in range(1, groups):
        ask_copy(step).start()

    def plane_copy(h, slot, d):
        return pltpu.make_async_remote_copy(
            src_ref=enc.at[2 * d + slot, h],
            dst_ref=cin.at[me, slot, h],
            send_sem=plane_send.at[h, slot, d],
            recv_sem=plane_recv.at[h, slot, me],
            device_id={"slab": d},
            device_id_type=MESH,
        )

    def plane_wait(h, slot, r):
        pltpu.make_async_remote_copy(
            src_ref=enc.at[slot, h],
            dst_ref=cin.at[r, slot, h],
            send_sem=plane_send.at[h, slot, r],
            recv_sem=plane_recv.at[h, slot, r],
            device_id={"slab": r},
            device_id_type=MESH,
        ).wait_recv()

    def forward_up(h, r):
        return pltpu.make_async_remote_copy(
            src_ref=cin.at[r, 2, h],
            dst_ref=cin.at[r, 0, h],
            send_sem=fwd_send.at[h, 0, r],
            recv_sem=plane_recv.at[h, 0, r],
            device_id={"slab": lax.rem(me + 1, slabs)},
            device_id_type=MESH,
        )

    def forward_down(h, r):
        return pltpu.make_async_remote_copy(
            src_ref=cin.at[r, 1, h],
            dst_ref=cin.at[r, 3, h],
            send_sem=fwd_send.at[h, 1, r],
            recv_sem=plane_recv.at[h, 3, r],
            device_id={"slab": lax.rem(me + slabs - 1, slabs)},
            device_id_type=MESH,
        )

    ups = (me != slabs - 1) & (me != half - 1)
    downs = (me != 0) & (me != half)

    def cond_copy(step):
        to = lax.rem(me + step, slabs)
        return pltpu.make_async_remote_copy(
            src_ref=cond_code.at[pl.ds(to * 2, 2)],
            dst_ref=cond_in.at[:, my_rows, :],
            send_sem=cond_send.at[step],
            recv_sem=cond_recv.at[step],
            device_id={"slab": to},
            device_id_type=MESH,
        )

    own_cond = pltpu.make_async_copy(cond_code.at[pl.ds(me * 2, 2)], cond_in.at[:, my_rows, :], local.at[1])

    def own_planes(h):
        return pltpu.make_async_copy(enc.at[pl.ds(2 * me, 4), h], cin.at[me, :, h], local.at[4 + h])

    cond_load.wait()

    @pl.loop(0, depth)
    def _(z):
        level = (cond_v[z] - COND_MID) * COND_STEPS
        level = level + jnp.where(level < 0, -0.5, 0.5)
        cond_code[z] = level.astype(jnp.int32).astype(jnp.int16)

    for step in range(1, slabs):
        cond_copy(step).start()
    own_cond.start()

    for step in range(1, groups):
        ask_copy(step).wait_recv()
    asked_copy = pltpu.make_async_copy(asked_in, asked_s, local.at[2])
    asked_copy.start()

    e_row = lax.broadcasted_iota(jnp.int32, (count, width), 0)
    lane = lax.broadcasted_iota(jnp.int32, (count, width), 1)
    hits = jnp.zeros((count, width), jnp.int32)
    for step in range(1, groups):
        wanted = jnp.broadcast_to(asked_in[step, 0:1, :], (count, width))
        hits = hits + jnp.where((wanted == e_row) & (lane < REQ), 1, 0)
    mark = jnp.broadcast_to(jnp.minimum(jnp.sum(hits, axis=1, keepdims=True), 1), (count, width))
    total = jnp.sum(mark, axis=0, keepdims=True)
    before = jnp.sum(jnp.where(e_row < lane, mark, 0), axis=0, keepdims=True)
    here = jnp.sum(jnp.where(e_row == lane, mark, 0), axis=0, keepdims=True)
    place = jnp.where(here > 0, before, total + lane[0:1] - before)
    across = jnp.broadcast_to(place, (count, width))
    down = jnp.sum(jnp.where(e_row == lane, across, 0), axis=1, keepdims=True)
    order = jnp.sum(jnp.where(jnp.broadcast_to(down, (count, width)) == lane, e_row, 0), axis=0, keepdims=True)
    eight = lax.broadcasted_iota(jnp.int32, (8, width), 0)
    place_v[...] = jnp.where(eight == 0, jnp.broadcast_to(place, (8, width)), jnp.broadcast_to(order, (8, width)))
    place_copy = pltpu.make_async_copy(place_v, place_s, local.at[3])
    place_copy.start()
    asked_copy.wait()
    place_copy.wait()
    for copy in loads:
        copy.wait()

    def edge_copies(h, d, act):
        close = d // half == upper

        @pl.when((d > 0) & (close | (d == half)))
        def _():
            act(plane_copy(h, 0, d))

        @pl.when((d < slabs - 1) & (close | (d == half - 1)))
        def _():
            act(plane_copy(h, 3, d))

    facing = jnp.where(upper == 0, half, half - 1)

    @pl.loop(0, 8)
    def _(n):
        h, kind = n // 4, lax.rem(n, 4)
        d0 = jnp.where(kind < 2, far0, near0)
        z0 = 2 * d0 + lax.rem(kind, 2)

        @pl.loop(0, some)
        def _(j):
            e = place_s[1, h * some + j]
            for q in range(half):
                stage[q, pl.ds(j, rows, stride=some), :] = pot_v[e, z0 + 2 * q]

        reached = [jnp.zeros((some, width), jnp.float32)] * half
        for slot in range(slots):
            for q in range(half):
                code = encode(stage[q, pl.ds(max(slot - 1, 0) * some, some), :] - reached[q])
                enc[z0 + 2 * q + 1, h, slot] = code
                reached[q] = reached[q] + decode(code)

        @pl.when(kind < 2)
        def _():
            @pl.loop(0, half)
            def _(q):
                plane_copy(h, 1 + kind, far0 + q).start()

        @pl.when(kind == 3)
        def _():
            edge_copies(h, facing, lambda copy: copy.start())
            own_planes(h).start()

            @pl.loop(0, half)
            def _(q):
                @pl.when(near0 + q != me)
                def _():
                    plane_copy(h, 1, near0 + q).start()
                    plane_copy(h, 2, near0 + q).start()
                    edge_copies(h, near0 + q, lambda copy: copy.start())

    def decode_plane(h, r, slot):
        reached = jnp.zeros((some, width), jnp.float32)
        for k in range(slots):
            reached = reached + decode(cin[r, slot, h, k])
            if k > 0:
                start = (slot * count + h * some) * tall + 8 + r * rows + k - 1
                field[pl.ds(start, some, stride=tall), :] = reached

    row_lane = lax.broadcasted_iota(jnp.int32, (rows, width), 1)

    def gradients(h, b, flat, steep):
        @pl.loop(h * some, (h + 1) * some)
        def _(e):
            def at(slot, shift):
                return field[pl.ds((slot * count + e) * tall + 8 + b * rows + shift, rows), :]

            for i in steep:
                own[b, e, 0, i] = ((at(2 + i, 0) - at(i, 0)) * 0.5).astype(jnp.bfloat16)
            for i in flat:
                here = at(1 + i, 0)
                right = jnp.where(row_lane < width - 1, pltpu.roll(here, width - 1, 1), 0.0)
                left = jnp.where(row_lane > 0, pltpu.roll(here, 1, 1), 0.0)
                own[b, e, 1, i] = ((at(1 + i, 1) - at(1 + i, -1)) * 0.5).astype(jnp.bfloat16)
                own[b, e, 2, i] = ((right - left) * 0.5).astype(jnp.bfloat16)

    def far_copy(k, step):
        return pltpu.make_async_remote_copy(
            src_ref=box.at[k, step - 1],
            dst_ref=far[k].at[pl.ds((groups - 1 - step) * REQ, REQ)],
            send_sem=far_send.at[k, step],
            recv_sem=far_recv.at[k, step],
            device_id={"elec": lax.rem(group + step, groups)},
            device_id_type=MESH,
        )

    def offer(k, b):
        for step in range(1, groups):
            for which in range(REQ):
                chosen = place_s[0, asked_s[groups - step, 0, which]]
                box[k, step - 1, which] = own[b, chosen]
            far_copy(k, step).start()

    def finish(k, b):
        for step in range(1, groups):
            far_copy(k, step).wait_recv()
        cut = pl.ds(pl.multiple_of(b * rows, rows), rows)
        weights = []
        for i in range(2):
            level = cond_in[i, cut, :].astype(jnp.int32).astype(jnp.float32)
            weights.append(-(level * (1.0 / COND_STEPS) + COND_MID))

        @pl.loop(0, readings // 4)
        def _(block):
            for n in range(4):
                m = block * 4 + n
                first, second = place_s[0, index[4 * m]], place_s[0, index[4 * m + 1]]
                third, fourth = index[4 * m + 2], index[4 * m + 3]
                for i in range(2):
                    total = None
                    for way in range(3):
                        source = minus(own[b, first, way, i], own[b, second, way, i])
                        probe = minus(far[k][third, way, i], far[k][fourth, way, i])
                        total = source * probe if total is None else total + source * probe
                    out[m, i, cut, :] = (weights[i] * total).astype(jnp.bfloat16)

    def take_near(h):
        @pl.loop(0, half)
        def _(j):
            r = near0 + j

            @pl.when(r == me)
            def _():
                own_planes(h).wait()

            @pl.when(r != me)
            def _():
                plane_wait(h, 1, r)
                plane_wait(h, 2, r)

                @pl.when(me > 0)
                def _():
                    plane_wait(h, 0, r)

                @pl.when(me < slabs - 1)
                def _():
                    plane_wait(h, 3, r)

            @pl.loop(0, 4)
            def _(slot):
                decode_plane(h, r, slot)

    def take_far(h, slot):
        @pl.loop(0, half)
        def _(j):
            r = far0 + j
            plane_wait(h, slot, r)

            @pl.when(downs if slot == 1 else ups)
            def _():
                (forward_down if slot == 1 else forward_up)(h, r).start()

            decode_plane(h, r, slot)

    def take_edges(h):
        @pl.loop(0, half)
        def _(j):
            r = far0 + j

            @pl.when(me < slabs - 1)
            def _():
                plane_wait(h, 3, r)

            decode_plane(h, r, 3)

            @pl.when(me > 0)
            def _():
                plane_wait(h, 0, r)

            decode_plane(h, r, 0)

    inside = upper * (half + 1)
    beyond = (1 - upper) * (half - 1)
    both = (0, 1)

    def each(start, number, act):
        @pl.loop(0, number)
        def _(j):
            act(start + j)

    take_near(0)
    take_far(0, 1)
    each(inside, half - 1, lambda b: gradients(0, b, both, both))
    for k in range(half - 1):
        offer(k, inside + k)
    take_far(0, 2)
    take_near(1)
    take_edges(0)
    each(beyond, half + 1, lambda b: gradients(0, b, both, both))
    for k in range(half + 1):
        offer(half - 1 + k, beyond + k)
    each(inside, half - 1, lambda b: gradients(1, b, both, both))
    for step in range(1, slabs):
        cond_copy(step).wait_recv()
    own_cond.wait()
    for k in range(half - 1):
        finish(k, inside + k)
    take_far(1, 1)
    each(beyond, half + 1, lambda b: gradients(1, b, (0,), ()))
    take_far(1, 2)
    each(beyond, half + 1, lambda b: gradients(1, b, (1,), ()))
    take_edges(1)
    each(beyond, half + 1, lambda b: gradients(1, b, (), both))
    for k in range(half + 1):
        finish(half - 1 + k, beyond + k)

    @pl.loop(0, slabs)
    def _(d):
        for h in range(2):

            @pl.when(d != me)
            def _(h=h):
                plane_copy(h, 1, d).wait_send()
                plane_copy(h, 2, d).wait_send()
                edge_copies(h, d, lambda copy: copy.wait_send())

            @pl.when((d // half != upper) & ups)
            def _(h=h):
                forward_up(h, d).wait_send()

            @pl.when((d // half != upper) & downs)
            def _(h=h):
                forward_down(h, d).wait_send()

    for step in range(1, slabs):
        cond_copy(step).wait_send()
    for step in range(1, groups):
        ask_copy(step).wait_send()
    for k in range(slabs):
        for step in range(1, groups):
            far_copy(k, step).wait_send()


def exchange(potentials, conductivity, asked, index, slabs, groups):
    count, depth, rows, width = potentials.shape
    readings = index.shape[0]
    x_size = rows * slabs
    anywhere = pl.BlockSpec(memory_space=pl.ANY)
    dma = pltpu.SemaphoreType.DMA
    bf16, f32, i16, i32 = jnp.bfloat16, jnp.float32, jnp.int16, jnp.int32
    asks = (groups - 1) * REQ
    return pl.pallas_call(
        functools.partial(exchange_kernel, slabs, groups),
        out_shape=pltpu.VMEM((readings, 2, x_size, width), bf16),
        in_specs=[anywhere, anywhere, pl.BlockSpec(memory_space=pltpu.VMEM), pl.BlockSpec(memory_space=pltpu.SMEM)],
        out_specs=pl.BlockSpec(memory_space=pltpu.VMEM),
        scratch_shapes=[
            pltpu.VMEM((count, depth, rows, width), f32),
            pltpu.VMEM((depth, rows, width), f32),
            pltpu.VMEM((slabs // 2, rows * count // 2, width), f32),
            pltpu.VMEM((depth + 2, 2, rows + 1, count // 2, width), i16),
            pltpu.VMEM((slabs, 4, 2, rows + 1, count // 2, width), i16),
            pltpu.VMEM((4 * count * (x_size + 16), width), f32),
            pltpu.VMEM((depth, rows, width), i16),
            pltpu.VMEM((2, x_size, width), i16),
            pltpu.VMEM((groups, 8, 128), i32),
            pltpu.SMEM((groups, 8, 128), i32),
            pltpu.VMEM((8, 128), i32),
            pltpu.SMEM((8, 128), i32),
            pltpu.VMEM((slabs, count, 3, 2, rows, width), bf16),
            pltpu.VMEM((slabs, groups - 1, REQ, 3, 2, rows, width), bf16),
        ]
        + [pltpu.VMEM((asks, 3, 2, rows, width), bf16)] * slabs
        + [
            dma((2, 4, slabs)),
            dma((2, 4, slabs)),
            dma((2, 2, slabs)),
            dma((slabs,)),
            dma((slabs,)),
            dma((groups,)),
            dma((groups,)),
            dma((slabs, groups)),
            dma((slabs, groups)),
            dma((PARTS,)),
            dma((6,)),
        ],
        compiler_params=pltpu.CompilerParams(
            collective_id=0, has_side_effects=True, vmem_limit_bytes=50 * 1024 * 1024
        ),
        name="exchange",
    )(potentials, conductivity, asked, index.reshape(-1))


def deliver_kernel(source, target, done):
    share = source.shape[0] // PARTS
    copies = [
        pltpu.make_async_copy(source.at[pl.ds(k * share, share)], target.at[pl.ds(k * share, share)], done.at[k])
        for k in range(PARTS)
    ]
    for copy in copies:
        copy.start()
    for copy in copies:
        copy.wait()


def deliver(rows):
    return pl.pallas_call(
        deliver_kernel,
        out_shape=jax.ShapeDtypeStruct(rows.shape, rows.dtype),
        in_specs=[pl.BlockSpec(memory_space=pl.ANY)],
        out_specs=pl.BlockSpec(memory_space=pl.ANY),
        scratch_shapes=[pltpu.SemaphoreType.DMA((PARTS,))],
        compiler_params=pltpu.CompilerParams(vmem_limit_bytes=1024 * 1024),
        name="deliver",
    )(rows)


def general(potentials, conductivity, quadrupoles):
    shifted = lax.all_to_all(potentials, "slab", split_axis=1, concat_axis=2, tiled=True)
    cond = lax.all_to_all(conductivity[None], "slab", split_axis=1, concat_axis=2, tiled=True)[0]
    slabs = lax.axis_size("slab")
    ends = slabs - 1
    last = shifted.shape[1] - 1
    below = lax.ppermute(shifted[:, last:], "slab", [(i, i + 1) for i in range(ends)])
    above = lax.ppermute(shifted[:, :1], "slab", [(i + 1, i) for i in range(ends)])
    tall = jnp.concatenate([below, shifted, above], axis=1)
    wide = jnp.pad(shifted, ((0, 0), (0, 0), (1, 1), (1, 1)))
    grads = jnp.stack(
        [
            (tall[:, 2:] - tall[:, :-2]) * 0.5,
            (wide[:, :, 2:, 1:-1] - wide[:, :, :-2, 1:-1]) * 0.5,
            (wide[:, :, 1:-1, 2:] - wide[:, :, 1:-1, :-2]) * 0.5,
        ],
        1,
    ).astype(jnp.bfloat16)
    table = lax.all_gather(grads.reshape(grads.shape[0], 3, -1), "elec", axis=0, tiled=True)
    ids = jnp.arange(table.shape[0], dtype=jnp.int32)
    hot = (quadrupoles[:, :, None] == ids).astype(jnp.bfloat16)
    flat = table.reshape(table.shape[0], -1)
    shape = (quadrupoles.shape[0], 3, -1)
    source = jnp.dot(hot[:, 0] - hot[:, 1], flat, preferred_element_type=jnp.float32).reshape(shape)
    probe = jnp.dot(hot[:, 2] - hot[:, 3], flat, preferred_element_type=jnp.float32).reshape(shape)
    rows = -(cond.reshape(-1)[None] * jnp.sum(source * probe, axis=1))
    return rows.astype(jnp.bfloat16).reshape((quadrupoles.shape[0],) + shifted.shape[1:])


def shards(potentials, conductivity, quadrupoles):
    slabs, groups = lax.axis_size("slab"), lax.axis_size("elec")
    count, depth, rows, width = potentials.shape
    fits = rows == 16 and width == 128 and depth == 2 * slabs and slabs % 4 == 0
    if not fits or count % 32 or 2 * (groups - 1) * REQ > count or count > 128 or quadrupoles.shape[0] % 4:
        return general(potentials, conductivity, quadrupoles)
    index, asked = lists(quadrupoles, count, groups)
    return deliver(exchange(potentials, conductivity, asked, index, slabs, groups))


def solution(mesh):
    in_specs = (P("elec", None, "slab", None), P(None, "slab", None), P("elec", None))
    out_specs = P("elec", "slab", None, None)
    return jax.shard_map(shards, mesh=mesh, in_specs=in_specs, out_specs=out_specs, check_vma=False)
```

```python
import functools

import jax
import jax.numpy as jnp
from jax import lax
from jax.experimental import pallas as pl
from jax.experimental.pallas import tpu as pltpu
from jax.sharding import PartitionSpec as P

MESH = pl.DeviceIdType.MESH
REQ = 4
PARTS = 4
SPAN = 12.5
LEVELS = 32767.0
GROUP = 8
COND_MID = 0.55
COND_STEPS = 32766.0 / 0.45


def lists(quadrupoles, per_group, groups):
    me = lax.axis_index("elec")
    ids = jnp.arange(per_group * groups, dtype=jnp.int32)
    owner = ids // per_group
    away = (owner - me) % groups
    named = jnp.any(quadrupoles[:, 2:4].reshape(-1)[:, None] == ids[None, :], axis=0)
    before = (owner[:, None] == owner[None, :]) & (ids[None, :] < ids[:, None])
    rank = jnp.sum((before & named[None, :]).astype(jnp.int32), axis=1)
    other = (away - 1) * REQ + jnp.minimum(rank, REQ - 1)
    slot = jnp.where(away == 0, ids - me * per_group, other)
    index = jnp.sum(jnp.where(quadrupoles[:, :, None] == ids, slot, 0), axis=-1)
    steps = jnp.arange(groups, dtype=jnp.int32)[:, None, None]
    lanes = jnp.arange(128, dtype=jnp.int32)[None, :, None]
    hit = named & (away == steps) & (rank == lanes)
    asked = jnp.sum(jnp.where(hit, ids % per_group, 0), axis=-1)
    return index.astype(jnp.int32), jnp.broadcast_to(asked[:, None, :], (groups, 8, 128))


def minus(first, second):
    return (first - second).astype(jnp.float32)


def decode(code):
    root = code.astype(jnp.int32).astype(jnp.float32) * (SPAN**0.125 / LEVELS)
    square = root * root
    fourth = square * square
    return (root * jnp.abs(root)) * square * fourth


def encode(step):
    level = jnp.exp2(jnp.log2(jnp.abs(step) * (1.0 / SPAN)) * 0.125) * LEVELS
    level = (level + 0.5).astype(jnp.int32)
    return jnp.where(step < 0, -level, level).astype(jnp.int16)


def exchange_kernel(slabs, groups, *refs):
    pot, cond, asked, index, out = refs[:5]
    pot_v, cond_v, stage, enc, cin, field, cond_code, cond_in = refs[5:13]
    asked_in, asked_s, place_v, place_s, own, box = refs[13:19]
    far = refs[19 : 19 + slabs]
    plane_send, plane_recv, fwd_send, cond_send, cond_recv = refs[19 + slabs : 24 + slabs]
    ask_send, ask_recv, far_send, far_recv, pot_sem, local = refs[24 + slabs :]

    count, depth, rows, width = pot.shape
    slots = rows + 1
    some = count // 2
    half = slabs // 2
    x_size = rows * slabs
    tall = x_size + 16
    readings = out.shape[0]
    me = lax.axis_index("slab")
    group = lax.axis_index("elec")
    upper = me // half
    near0 = upper * half
    far0 = (1 - upper) * half
    my_rows = pl.ds(pl.multiple_of(me * rows, rows), rows)

    share = count // PARTS
    loads = [
        pltpu.make_async_copy(pot.at[pl.ds(k * share, share)], pot_v.at[pl.ds(k * share, share)], pot_sem.at[k])
        for k in range(PARTS)
    ]
    cond_load = pltpu.make_async_copy(cond, cond_v, local.at[0])

    barrier = pltpu.get_barrier_semaphore()
    for step in range(1, groups):
        pl.semaphore_signal(barrier, inc=1, device_id={"elec": lax.rem(group + step, groups)}, device_id_type=MESH)
    for step in range(1, slabs):
        pl.semaphore_signal(barrier, inc=1, device_id={"slab": lax.rem(me + step, slabs)}, device_id_type=MESH)
    for copy in loads:
        copy.start()
    cond_load.start()

    blank = jnp.zeros((2, slots, some, width), jnp.int16)
    enc[0] = blank
    enc[depth + 1] = blank

    @pl.when(me == 0)
    def _():
        @pl.loop(1, slabs)
        def _(r):
            cin[r, 0] = blank

    @pl.when(me == slabs - 1)
    def _():
        @pl.loop(0, slabs - 1)
        def _(r):
            cin[r, 3] = blank

    @pl.loop(0, 2 * count)
    def _(k):
        base = (count + k) * tall
        edge = jnp.zeros((8, width), jnp.float32)
        field[pl.ds(pl.multiple_of(base, 8), 8), :] = edge
        field[pl.ds(pl.multiple_of(base + tall - 8, 8), 8), :] = edge

    pl.semaphore_wait(barrier, slabs + groups - 2)

    def ask_copy(step):
        return pltpu.make_async_remote_copy(
            src_ref=asked.at[step],
            dst_ref=asked_in.at[step],
            send_sem=ask_send.at[step],
            recv_sem=ask_recv.at[step],
            device_id={"elec": lax.rem(group + step, groups)},
            device_id_type=MESH,
        )

    for step in range(1, groups):
        ask_copy(step).start()

    def plane_copy(h, slot, d):
        return pltpu.make_async_remote_copy(
            src_ref=enc.at[2 * d + slot, h],
            dst_ref=cin.at[me, slot, h],
            send_sem=plane_send.at[h, slot, d],
            recv_sem=plane_recv.at[h, slot, me],
            device_id={"slab": d},
            device_id_type=MESH,
        )

    def plane_wait(h, slot, r):
        pltpu.make_async_remote_copy(
            src_ref=enc.at[slot, h],
            dst_ref=cin.at[r, slot, h],
            send_sem=plane_send.at[h, slot, r],
            recv_sem=plane_recv.at[h, slot, r],
            device_id={"slab": r},
            device_id_type=MESH,
        ).wait_recv()

    def forward_up(h, r):
        return pltpu.make_async_remote_copy(
            src_ref=cin.at[r, 2, h],
            dst_ref=cin.at[r, 0, h],
            send_sem=fwd_send.at[h, 0, r],
            recv_sem=plane_recv.at[h, 0, r],
            device_id={"slab": lax.rem(me + 1, slabs)},
            device_id_type=MESH,
        )

    def forward_down(h, r):
        return pltpu.make_async_remote_copy(
            src_ref=cin.at[r, 1, h],
            dst_ref=cin.at[r, 3, h],
            send_sem=fwd_send.at[h, 1, r],
            recv_sem=plane_recv.at[h, 3, r],
            device_id={"slab": lax.rem(me + slabs - 1, slabs)},
            device_id_type=MESH,
        )

    ups = (me != slabs - 1) & (me != half - 1)
    downs = (me != 0) & (me != half)

    def cond_copy(step):
        to = lax.rem(me + step, slabs)
        return pltpu.make_async_remote_copy(
            src_ref=cond_code.at[pl.ds(to * 2, 2)],
            dst_ref=cond_in.at[:, my_rows, :],
            send_sem=cond_send.at[step],
            recv_sem=cond_recv.at[step],
            device_id={"slab": to},
            device_id_type=MESH,
        )

    own_cond = pltpu.make_async_copy(cond_code.at[pl.ds(me * 2, 2)], cond_in.at[:, my_rows, :], local.at[1])

    def own_planes(h):
        return pltpu.make_async_copy(enc.at[pl.ds(2 * me, 4), h], cin.at[me, :, h], local.at[4 + h])

    cond_load.wait()

    @pl.loop(0, depth)
    def _(z):
        level = (cond_v[z] - COND_MID) * COND_STEPS
        level = level + jnp.where(level < 0, -0.5, 0.5)
        cond_code[z] = level.astype(jnp.int32).astype(jnp.int16)

    for step in range(1, slabs):
        cond_copy(step).start()
    own_cond.start()

    for step in range(1, groups):
        ask_copy(step).wait_recv()
    asked_copy = pltpu.make_async_copy(asked_in, asked_s, local.at[2])
    asked_copy.start()

    e_row = lax.broadcasted_iota(jnp.int32, (count, width), 0)
    lane = lax.broadcasted_iota(jnp.int32, (count, width), 1)
    hits = jnp.zeros((count, width), jnp.int32)
    for step in range(1, groups):
        wanted = jnp.broadcast_to(asked_in[step, 0:1, :], (count, width))
        hits = hits + jnp.where((wanted == e_row) & (lane < REQ), 1, 0)
    mark = jnp.broadcast_to(jnp.minimum(jnp.sum(hits, axis=1, keepdims=True), 1), (count, width))
    total = jnp.sum(mark, axis=0, keepdims=True)
    before = jnp.sum(jnp.where(e_row < lane, mark, 0), axis=0, keepdims=True)
    here = jnp.sum(jnp.where(e_row == lane, mark, 0), axis=0, keepdims=True)
    place = jnp.where(here > 0, before, total + lane[0:1] - before)
    across = jnp.broadcast_to(place, (count, width))
    down = jnp.sum(jnp.where(e_row == lane, across, 0), axis=1, keepdims=True)
    order = jnp.sum(jnp.where(jnp.broadcast_to(down, (count, width)) == lane, e_row, 0), axis=0, keepdims=True)
    eight = lax.broadcasted_iota(jnp.int32, (8, width), 0)
    place_v[...] = jnp.where(eight == 0, jnp.broadcast_to(place, (8, width)), jnp.broadcast_to(order, (8, width)))
    place_copy = pltpu.make_async_copy(place_v, place_s, local.at[3])
    place_copy.start()
    asked_copy.wait()
    place_copy.wait()
    for copy in loads:
        copy.wait()

    def edge_copies(h, d, act):
        close = d // half == upper

        @pl.when((d > 0) & (close | (d == half)))
        def _():
            act(plane_copy(h, 0, d))

        @pl.when((d < slabs - 1) & (close | (d == half - 1)))
        def _():
            act(plane_copy(h, 3, d))

    facing = jnp.where(upper == 0, half, half - 1)

    def send_near(h):
        own_planes(h).start()

        @pl.loop(0, half)
        def _(q):
            @pl.when(near0 + q != me)
            def _():
                plane_copy(h, 1, near0 + q).start()
                plane_copy(h, 2, near0 + q).start()
                edge_copies(h, near0 + q, lambda copy: copy.start())

    @pl.loop(0, 8)
    def _(n):
        h, kind = n // 4, lax.rem(n, 4)
        d0 = jnp.where(kind < 2, far0, near0)
        z0 = 2 * d0 + lax.rem(kind, 2)

        @pl.loop(0, some)
        def _(j):
            e = place_s[1, h * some + j]
            for q in range(half):
                stage[q, pl.ds(j, rows, stride=some), :] = pot_v[e, z0 + 2 * q]

        reached = [jnp.zeros((some, width), jnp.float32)] * half
        for slot in range(slots):
            for q in range(half):
                code = encode(stage[q, pl.ds(max(slot - 1, 0) * some, some), :] - reached[q])
                enc[z0 + 2 * q + 1, h, slot] = code
                reached[q] = reached[q] + decode(code)

        @pl.when(kind < 2)
        def _():
            @pl.loop(0, half)
            def _(q):
                plane_copy(h, 1 + kind, far0 + q).start()

        @pl.when(kind == 3)
        def _():
            edge_copies(h, facing, lambda copy: copy.start())

        @pl.when(n == 3)
        def _():
            send_near(0)

    def decode_plane(h, r, slot):
        reached = jnp.zeros((some, width), jnp.float32)
        for k in range(slots):
            reached = reached + decode(cin[r, slot, h, k])
            if k > 0:
                start = (slot * count + h * some) * tall + 8 + r * rows + k - 1
                field[pl.ds(start, some, stride=tall), :] = reached

    row_lane = lax.broadcasted_iota(jnp.int32, (rows, width), 1)

    def gradients(h, b, flat, steep):
        @pl.loop(0, some // GROUP)
        def _(n):
            for e in [h * some + n * GROUP + g for g in range(GROUP)]:

                def at(slot, shift, e=e):
                    return field[pl.ds((slot * count + e) * tall + 8 + b * rows + shift, rows), :]

                for i in steep:
                    own[b, e, 0, i] = ((at(2 + i, 0) - at(i, 0)) * 0.5).astype(jnp.bfloat16)
                for i in flat:
                    here = at(1 + i, 0)
                    right = jnp.where(row_lane < width - 1, pltpu.roll(here, width - 1, 1), 0.0)
                    left = jnp.where(row_lane > 0, pltpu.roll(here, 1, 1), 0.0)
                    own[b, e, 1, i] = ((at(1 + i, 1) - at(1 + i, -1)) * 0.5).astype(jnp.bfloat16)
                    own[b, e, 2, i] = ((right - left) * 0.5).astype(jnp.bfloat16)

    def far_copy(k, step):
        return pltpu.make_async_remote_copy(
            src_ref=box.at[k, step - 1],
            dst_ref=far[k].at[pl.ds((groups - 1 - step) * REQ, REQ)],
            send_sem=far_send.at[k, step],
            recv_sem=far_recv.at[k, step],
            device_id={"elec": lax.rem(group + step, groups)},
            device_id_type=MESH,
        )

    def offer(k, b):
        for step in range(1, groups):
            for which in range(REQ):
                chosen = place_s[0, asked_s[groups - step, 0, which]]
                box[k, step - 1, which] = own[b, chosen]
            far_copy(k, step).start()

    def finish(k, b):
        for step in range(1, groups):
            far_copy(k, step).wait_recv()
        cut = pl.ds(pl.multiple_of(b * rows, rows), rows)
        weight = -(cond_in[:, cut, :].astype(jnp.int32).astype(jnp.float32) * (1.0 / COND_STEPS) + COND_MID)

        @pl.loop(0, readings // 8)
        def _(block):
            for n in range(8):
                m = block * 8 + n
                first, second = place_s[0, index[4 * m]], place_s[0, index[4 * m + 1]]
                third, fourth = index[4 * m + 2], index[4 * m + 3]
                product = minus(own[b, first], own[b, second]) * minus(far[k][third], far[k][fourth])
                out[m, :, cut, :] = (weight * (product[0] + product[1] + product[2])).astype(jnp.bfloat16)

    def take_near(h):
        @pl.loop(0, half)
        def _(j):
            r = near0 + j

            @pl.when(r == me)
            def _():
                own_planes(h).wait()

            @pl.when(r != me)
            def _():
                plane_wait(h, 1, r)
                plane_wait(h, 2, r)

                @pl.when(me > 0)
                def _():
                    plane_wait(h, 0, r)

                @pl.when(me < slabs - 1)
                def _():
                    plane_wait(h, 3, r)

            @pl.loop(0, 4)
            def _(slot):
                decode_plane(h, r, slot)

    def take_far(h, slot):
        @pl.loop(0, half)
        def _(j):
            r = far0 + j
            plane_wait(h, slot, r)

            @pl.when(downs if slot == 1 else ups)
            def _():
                (forward_down if slot == 1 else forward_up)(h, r).start()

            decode_plane(h, r, slot)

    def take_edges(h):
        @pl.loop(0, half)
        def _(j):
            r = far0 + j

            @pl.when(me < slabs - 1)
            def _():
                plane_wait(h, 3, r)

            decode_plane(h, r, 3)

            @pl.when(me > 0)
            def _():
                plane_wait(h, 0, r)

            decode_plane(h, r, 0)

    inside = upper * (half + 1)
    beyond = (1 - upper) * (half - 1)
    both = (0, 1)

    def each(start, number, act):
        @pl.loop(0, number)
        def _(j):
            act(start + j)

    take_far(0, 1)
    take_near(0)
    each(inside, half - 1, lambda b: gradients(0, b, both, both))
    for k in range(half - 1):
        offer(k, inside + k)
    take_far(0, 2)
    send_near(1)
    take_edges(0)
    each(beyond, half + 1, lambda b: gradients(0, b, both, both))
    for k in range(half + 1):
        offer(half - 1 + k, beyond + k)
    take_far(1, 1)
    take_near(1)
    each(inside, half - 1, lambda b: gradients(1, b, both, both))
    each(beyond, half + 1, lambda b: gradients(1, b, (0,), ()))
    take_far(1, 2)
    for step in range(1, slabs):
        cond_copy(step).wait_recv()
    own_cond.wait()
    for k in range(half - 1):
        finish(k, inside + k)
    each(beyond, half + 1, lambda b: gradients(1, b, (1,), ()))
    take_edges(1)
    each(beyond, half + 1, lambda b: gradients(1, b, (), both))
    for k in range(half + 1):
        finish(half - 1 + k, beyond + k)

    @pl.loop(0, slabs)
    def _(d):
        for h in range(2):

            @pl.when(d != me)
            def _(h=h):
                plane_copy(h, 1, d).wait_send()
                plane_copy(h, 2, d).wait_send()
                edge_copies(h, d, lambda copy: copy.wait_send())

            @pl.when((d // half != upper) & ups)
            def _(h=h):
                forward_up(h, d).wait_send()

            @pl.when((d // half != upper) & downs)
            def _(h=h):
                forward_down(h, d).wait_send()

    for step in range(1, slabs):
        cond_copy(step).wait_send()
    for step in range(1, groups):
        ask_copy(step).wait_send()
    for k in range(slabs):
        for step in range(1, groups):
            far_copy(k, step).wait_send()


def exchange(potentials, conductivity, asked, index, slabs, groups):
    count, depth, rows, width = potentials.shape
    readings = index.shape[0]
    x_size = rows * slabs
    anywhere = pl.BlockSpec(memory_space=pl.ANY)
    dma = pltpu.SemaphoreType.DMA
    bf16, f32, i16, i32 = jnp.bfloat16, jnp.float32, jnp.int16, jnp.int32
    asks = (groups - 1) * REQ
    return pl.pallas_call(
        functools.partial(exchange_kernel, slabs, groups),
        out_shape=pltpu.VMEM((readings, 2, x_size, width), bf16),
        in_specs=[anywhere, anywhere, pl.BlockSpec(memory_space=pltpu.VMEM), pl.BlockSpec(memory_space=pltpu.SMEM)],
        out_specs=pl.BlockSpec(memory_space=pltpu.VMEM),
        scratch_shapes=[
            pltpu.VMEM((count, depth, rows, width), f32),
            pltpu.VMEM((depth, rows, width), f32),
            pltpu.VMEM((slabs // 2, rows * count // 2, width), f32),
            pltpu.VMEM((depth + 2, 2, rows + 1, count // 2, width), i16),
            pltpu.VMEM((slabs, 4, 2, rows + 1, count // 2, width), i16),
            pltpu.VMEM((4 * count * (x_size + 16), width), f32),
            pltpu.VMEM((depth, rows, width), i16),
            pltpu.VMEM((2, x_size, width), i16),
            pltpu.VMEM((groups, 8, 128), i32),
            pltpu.SMEM((groups, 8, 128), i32),
            pltpu.VMEM((8, 128), i32),
            pltpu.SMEM((8, 128), i32),
            pltpu.VMEM((slabs, count, 3, 2, rows, width), bf16),
            pltpu.VMEM((slabs, groups - 1, REQ, 3, 2, rows, width), bf16),
        ]
        + [pltpu.VMEM((asks, 3, 2, rows, width), bf16)] * slabs
        + [
            dma((2, 4, slabs)),
            dma((2, 4, slabs)),
            dma((2, 2, slabs)),
            dma((slabs,)),
            dma((slabs,)),
            dma((groups,)),
            dma((groups,)),
            dma((slabs, groups)),
            dma((slabs, groups)),
            dma((PARTS,)),
            dma((6,)),
        ],
        compiler_params=pltpu.CompilerParams(
            collective_id=0, has_side_effects=True, vmem_limit_bytes=50 * 1024 * 1024
        ),
        name="exchange",
    )(potentials, conductivity, asked, index.reshape(-1))


def deliver_kernel(source, target, done):
    share = source.shape[0] // PARTS
    copies = [
        pltpu.make_async_copy(source.at[pl.ds(k * share, share)], target.at[pl.ds(k * share, share)], done.at[k])
        for k in range(PARTS)
    ]
    for copy in copies:
        copy.start()
    for copy in copies:
        copy.wait()


def deliver(rows):
    return pl.pallas_call(
        deliver_kernel,
        out_shape=jax.ShapeDtypeStruct(rows.shape, rows.dtype),
        in_specs=[pl.BlockSpec(memory_space=pl.ANY)],
        out_specs=pl.BlockSpec(memory_space=pl.ANY),
        scratch_shapes=[pltpu.SemaphoreType.DMA((PARTS,))],
        compiler_params=pltpu.CompilerParams(vmem_limit_bytes=1024 * 1024),
        name="deliver",
    )(rows)


def general(potentials, conductivity, quadrupoles):
    shifted = lax.all_to_all(potentials, "slab", split_axis=1, concat_axis=2, tiled=True)
    cond = lax.all_to_all(conductivity[None], "slab", split_axis=1, concat_axis=2, tiled=True)[0]
    slabs = lax.axis_size("slab")
    ends = slabs - 1
    last = shifted.shape[1] - 1
    below = lax.ppermute(shifted[:, last:], "slab", [(i, i + 1) for i in range(ends)])
    above = lax.ppermute(shifted[:, :1], "slab", [(i + 1, i) for i in range(ends)])
    tall = jnp.concatenate([below, shifted, above], axis=1)
    wide = jnp.pad(shifted, ((0, 0), (0, 0), (1, 1), (1, 1)))
    grads = jnp.stack(
        [
            (tall[:, 2:] - tall[:, :-2]) * 0.5,
            (wide[:, :, 2:, 1:-1] - wide[:, :, :-2, 1:-1]) * 0.5,
            (wide[:, :, 1:-1, 2:] - wide[:, :, 1:-1, :-2]) * 0.5,
        ],
        1,
    ).astype(jnp.bfloat16)
    table = lax.all_gather(grads.reshape(grads.shape[0], 3, -1), "elec", axis=0, tiled=True)
    ids = jnp.arange(table.shape[0], dtype=jnp.int32)
    hot = (quadrupoles[:, :, None] == ids).astype(jnp.bfloat16)
    flat = table.reshape(table.shape[0], -1)
    shape = (quadrupoles.shape[0], 3, -1)
    source = jnp.dot(hot[:, 0] - hot[:, 1], flat, preferred_element_type=jnp.float32).reshape(shape)
    probe = jnp.dot(hot[:, 2] - hot[:, 3], flat, preferred_element_type=jnp.float32).reshape(shape)
    rows = -(cond.reshape(-1)[None] * jnp.sum(source * probe, axis=1))
    return rows.astype(jnp.bfloat16).reshape((quadrupoles.shape[0],) + shifted.shape[1:])


def shards(potentials, conductivity, quadrupoles):
    slabs, groups = lax.axis_size("slab"), lax.axis_size("elec")
    count, depth, rows, width = potentials.shape
    fits = rows == 16 and width == 128 and depth == 2 * slabs and slabs % 4 == 0
    if not fits or count % 32 or 2 * (groups - 1) * REQ > count or count > 128 or quadrupoles.shape[0] % 8:
        return general(potentials, conductivity, quadrupoles)
    index, asked = lists(quadrupoles, count, groups)
    return deliver(exchange(potentials, conductivity, asked, index, slabs, groups))


def solution(mesh):
    in_specs = (P("elec", None, "slab", None), P(None, "slab", None), P("elec", None))
    out_specs = P("elec", "slab", None, None)
    return jax.shard_map(shards, mesh=mesh, in_specs=in_specs, out_specs=out_specs, check_vma=False)
```

```python
import functools

import jax
import jax.numpy as jnp
from jax import lax
from jax.experimental import pallas as pl
from jax.experimental.pallas import tpu as pltpu
from jax.sharding import PartitionSpec as P

MESH = pl.DeviceIdType.MESH
REQ = 4
PARTS = 4
SPAN = 12.5
LEVELS = 32767.0
GROUP = 8
COND_MID = 0.55
COND_STEPS = 32766.0 / 0.45


def minus(first, second):
    return (first - second).astype(jnp.float32)


def decode(code):
    root = code.astype(jnp.int32).astype(jnp.float32) * (SPAN**0.125 / LEVELS)
    square = root * root
    fourth = square * square
    return (root * jnp.abs(root)) * square * fourth


def encode(step):
    level = jnp.exp2(jnp.log2(jnp.abs(step) * (1.0 / SPAN)) * 0.125) * LEVELS
    level = (level + 0.5).astype(jnp.int32)
    return jnp.where(step < 0, -level, level).astype(jnp.int16)


def exchange_kernel(slabs, groups, *refs):
    pot, cond, quads, index, out = refs[:5]
    pot_v, cond_v, stage, enc, cin, field, cond_code, cond_in = refs[5:13]
    asked_in, asked_s, place_v, place_s, asked, spots, own, box = refs[13:21]
    far = refs[21 : 21 + slabs]
    plane_send, plane_recv, fwd_send, cond_send, cond_recv = refs[21 + slabs : 26 + slabs]
    ask_send, ask_recv, far_send, far_recv, pot_sem, local = refs[26 + slabs :]

    count, depth, rows, width = pot.shape
    slots = rows + 1
    some = count // 2
    half = slabs // 2
    x_size = rows * slabs
    tall = x_size + 16
    readings = out.shape[0]
    me = lax.axis_index("slab")
    group = lax.axis_index("elec")
    upper = me // half
    near0 = upper * half
    far0 = (1 - upper) * half
    my_rows = pl.ds(pl.multiple_of(me * rows, rows), rows)

    share = count // PARTS
    loads = [
        pltpu.make_async_copy(pot.at[pl.ds(k * share, share)], pot_v.at[pl.ds(k * share, share)], pot_sem.at[k])
        for k in range(PARTS)
    ]
    cond_load = pltpu.make_async_copy(cond, cond_v, local.at[0])

    barrier = pltpu.get_barrier_semaphore()
    for step in range(1, groups):
        pl.semaphore_signal(barrier, inc=1, device_id={"elec": lax.rem(group + step, groups)}, device_id_type=MESH)
    for step in range(1, slabs):
        pl.semaphore_signal(barrier, inc=1, device_id={"slab": lax.rem(me + step, slabs)}, device_id_type=MESH)
    for copy in loads:
        copy.start()
    cond_load.start()

    blank = jnp.zeros((2, slots, some, width), jnp.int16)
    enc[0] = blank
    enc[depth + 1] = blank

    @pl.when(me == 0)
    def _():
        @pl.loop(1, slabs)
        def _(r):
            cin[r, 0] = blank

    @pl.when(me == slabs - 1)
    def _():
        @pl.loop(0, slabs - 1)
        def _(r):
            cin[r, 3] = blank

    @pl.loop(0, 2 * count)
    def _(k):
        base = (count + k) * tall
        edge = jnp.zeros((8, width), jnp.float32)
        field[pl.ds(pl.multiple_of(base, 8), 8), :] = edge
        field[pl.ds(pl.multiple_of(base + tall - 8, 8), 8), :] = edge

    lane = lax.broadcasted_iota(jnp.int32, (width, width), 1)
    down_id = lax.broadcasted_iota(jnp.int32, (width, width), 0)

    def turned(flat):
        return jnp.broadcast_to(jnp.sum(jnp.where(down_id == lane, flat, 0), axis=1, keepdims=True), (width, width))

    ids = lax.broadcasted_iota(jnp.int32, (readings, width), 1)
    third, fourth = (jnp.broadcast_to(quads[:, c : c + 1], (readings, width)) for c in (2, 3))
    named = jnp.sum(jnp.where((third == ids) | (fourth == ids), 1, 0), axis=0, keepdims=True)
    named = turned(jnp.broadcast_to(jnp.minimum(named, 1), (width, width)))
    earlier = (lane // count == down_id // count) & (down_id < lane)
    rank = jnp.sum(jnp.where(earlier, named, 0), axis=0, keepdims=True)
    across = lane[0:1]
    away = lax.rem(across // count - group + groups, groups)
    spot = jnp.where(away == 0, 0, (away - 1) * REQ + jnp.minimum(rank, REQ - 1))
    rank_down = turned(jnp.broadcast_to(rank, (width, width)))
    away_down = lax.rem(down_id // count - group + groups, groups)
    for step in range(1, groups):
        hit = (named > 0) & (away_down == step) & (rank_down == lane)
        chosen = jnp.sum(jnp.where(hit, lax.rem(down_id, count), 0), axis=0, keepdims=True)
        asked[step] = jnp.broadcast_to(chosen, (8, width))

    pl.semaphore_wait(barrier, slabs + groups - 2)

    def ask_copy(step):
        return pltpu.make_async_remote_copy(
            src_ref=asked.at[step],
            dst_ref=asked_in.at[step],
            send_sem=ask_send.at[step],
            recv_sem=ask_recv.at[step],
            device_id={"elec": lax.rem(group + step, groups)},
            device_id_type=MESH,
        )

    for step in range(1, groups):
        ask_copy(step).start()

    def plane_copy(h, slot, d):
        return pltpu.make_async_remote_copy(
            src_ref=enc.at[2 * d + slot, h],
            dst_ref=cin.at[me, slot, h],
            send_sem=plane_send.at[h, slot, d],
            recv_sem=plane_recv.at[h, slot, me],
            device_id={"slab": d},
            device_id_type=MESH,
        )

    def plane_wait(h, slot, r):
        pltpu.make_async_remote_copy(
            src_ref=enc.at[slot, h],
            dst_ref=cin.at[r, slot, h],
            send_sem=plane_send.at[h, slot, r],
            recv_sem=plane_recv.at[h, slot, r],
            device_id={"slab": r},
            device_id_type=MESH,
        ).wait_recv()

    def forward_up(h, r):
        return pltpu.make_async_remote_copy(
            src_ref=cin.at[r, 2, h],
            dst_ref=cin.at[r, 0, h],
            send_sem=fwd_send.at[h, 0, r],
            recv_sem=plane_recv.at[h, 0, r],
            device_id={"slab": lax.rem(me + 1, slabs)},
            device_id_type=MESH,
        )

    def forward_down(h, r):
        return pltpu.make_async_remote_copy(
            src_ref=cin.at[r, 1, h],
            dst_ref=cin.at[r, 3, h],
            send_sem=fwd_send.at[h, 1, r],
            recv_sem=plane_recv.at[h, 3, r],
            device_id={"slab": lax.rem(me + slabs - 1, slabs)},
            device_id_type=MESH,
        )

    ups = (me != slabs - 1) & (me != half - 1)
    downs = (me != 0) & (me != half)

    def cond_copy(step):
        to = lax.rem(me + step, slabs)
        return pltpu.make_async_remote_copy(
            src_ref=cond_code.at[pl.ds(to * 2, 2)],
            dst_ref=cond_in.at[:, my_rows, :],
            send_sem=cond_send.at[step],
            recv_sem=cond_recv.at[step],
            device_id={"slab": to},
            device_id_type=MESH,
        )

    own_cond = pltpu.make_async_copy(cond_code.at[pl.ds(me * 2, 2)], cond_in.at[:, my_rows, :], local.at[1])

    def own_planes(h):
        return pltpu.make_async_copy(enc.at[pl.ds(2 * me, 4), h], cin.at[me, :, h], local.at[4 + h])

    cond_load.wait()

    @pl.loop(0, depth)
    def _(z):
        level = (cond_v[z] - COND_MID) * COND_STEPS
        level = level + jnp.where(level < 0, -0.5, 0.5)
        cond_code[z] = level.astype(jnp.int32).astype(jnp.int16)

    for step in range(1, slabs):
        cond_copy(step).start()
    own_cond.start()

    for step in range(1, groups):
        ask_copy(step).wait_recv()
    asked_copy = pltpu.make_async_copy(asked_in, asked_s, local.at[2])
    asked_copy.start()

    e_row = lax.broadcasted_iota(jnp.int32, (count, width), 0)
    lane = lax.broadcasted_iota(jnp.int32, (count, width), 1)
    hits = jnp.zeros((count, width), jnp.int32)
    for step in range(1, groups):
        wanted = jnp.broadcast_to(asked_in[step, 0:1, :], (count, width))
        hits = hits + jnp.where((wanted == e_row) & (lane < REQ), 1, 0)
    mark = jnp.broadcast_to(jnp.minimum(jnp.sum(hits, axis=1, keepdims=True), 1), (count, width))
    total = jnp.sum(mark, axis=0, keepdims=True)
    before = jnp.sum(jnp.where(e_row < lane, mark, 0), axis=0, keepdims=True)
    here = jnp.sum(jnp.where(e_row == lane, mark, 0), axis=0, keepdims=True)
    place = jnp.where(here > 0, before, total + lane[0:1] - before)
    across = jnp.broadcast_to(place, (count, width))
    down = jnp.sum(jnp.where(e_row == lane, across, 0), axis=1, keepdims=True)
    order = jnp.sum(jnp.where(jnp.broadcast_to(down, (count, width)) == lane, e_row, 0), axis=0, keepdims=True)
    eight = lax.broadcasted_iota(jnp.int32, (8, width), 0)
    table = jnp.where(eight == 0, jnp.broadcast_to(place, (8, width)), jnp.broadcast_to(order, (8, width)))
    place_v[...] = jnp.where(eight == 2, jnp.broadcast_to(spot, (8, width)), table)
    place_copy = pltpu.make_async_copy(place_v, place_s, local.at[3])
    place_copy.start()
    asked_copy.wait()
    place_copy.wait()
    for copy in loads:
        copy.wait()

    def edge_copies(h, d, act):
        close = d // half == upper

        @pl.when((d > 0) & (close | (d == half)))
        def _():
            act(plane_copy(h, 0, d))

        @pl.when((d < slabs - 1) & (close | (d == half - 1)))
        def _():
            act(plane_copy(h, 3, d))

    facing = jnp.where(upper == 0, half, half - 1)

    def send_near(h):
        own_planes(h).start()

        @pl.loop(0, half)
        def _(q):
            @pl.when(near0 + q != me)
            def _():
                plane_copy(h, 1, near0 + q).start()
                plane_copy(h, 2, near0 + q).start()
                edge_copies(h, near0 + q, lambda copy: copy.start())

    @pl.loop(0, 8)
    def _(n):
        h, kind = n // 4, lax.rem(n, 4)
        d0 = jnp.where(kind < 2, far0, near0)
        z0 = 2 * d0 + lax.rem(kind, 2)

        @pl.loop(0, some)
        def _(j):
            e = place_s[1, h * some + j]
            for q in range(half):
                stage[q, pl.ds(j, rows, stride=some), :] = pot_v[e, z0 + 2 * q]

        reached = [jnp.zeros((some, width), jnp.float32)] * half
        for slot in range(slots):
            for q in range(half):
                code = encode(stage[q, pl.ds(max(slot - 1, 0) * some, some), :] - reached[q])
                enc[z0 + 2 * q + 1, h, slot] = code
                reached[q] = reached[q] + decode(code)

        @pl.when(kind < 2)
        def _():
            @pl.loop(0, half)
            def _(q):
                plane_copy(h, 1 + kind, far0 + q).start()

        @pl.when(kind == 3)
        def _():
            edge_copies(h, facing, lambda copy: copy.start())

        @pl.when(n == 3)
        def _():
            send_near(0)

    @pl.loop(0, readings // 4)
    def _(block):
        for n in range(4):
            m = block * 4 + n
            for c in range(2):
                spots[4 * m + c] = place_s[0, lax.rem(index[4 * m + c], count)]
                spots[4 * m + 2 + c] = place_s[2, index[4 * m + 2 + c]]

    def decode_plane(h, r, slot):
        reached = jnp.zeros((some, width), jnp.float32)
        for k in range(slots):
            reached = reached + decode(cin[r, slot, h, k])
            if k > 0:
                start = (slot * count + h * some) * tall + 8 + r * rows + k - 1
                field[pl.ds(start, some, stride=tall), :] = reached

    row_lane = lax.broadcasted_iota(jnp.int32, (rows, width), 1)

    def gradients(h, b, flat, steep):
        @pl.loop(0, some // GROUP)
        def _(n):
            for e in [h * some + n * GROUP + g for g in range(GROUP)]:

                def at(slot, shift, e=e):
                    return field[pl.ds((slot * count + e) * tall + 8 + b * rows + shift, rows), :]

                for i in steep:
                    own[b, e, 0, i] = ((at(2 + i, 0) - at(i, 0)) * 0.5).astype(jnp.bfloat16)
                for i in flat:
                    here = at(1 + i, 0)
                    right = jnp.where(row_lane < width - 1, pltpu.roll(here, width - 1, 1), 0.0)
                    left = jnp.where(row_lane > 0, pltpu.roll(here, 1, 1), 0.0)
                    own[b, e, 1, i] = ((at(1 + i, 1) - at(1 + i, -1)) * 0.5).astype(jnp.bfloat16)
                    own[b, e, 2, i] = ((right - left) * 0.5).astype(jnp.bfloat16)

    def far_copy(k, step):
        return pltpu.make_async_remote_copy(
            src_ref=box.at[k, step - 1],
            dst_ref=far[k].at[pl.ds((groups - 1 - step) * REQ, REQ)],
            send_sem=far_send.at[k, step],
            recv_sem=far_recv.at[k, step],
            device_id={"elec": lax.rem(group + step, groups)},
            device_id_type=MESH,
        )

    def offer(k, b):
        for step in range(1, groups):
            for which in range(REQ):
                chosen = place_s[0, asked_s[groups - step, 0, which]]
                box[k, step - 1, which] = own[b, chosen]
            far_copy(k, step).start()

    def finish(k, b):
        for step in range(1, groups):
            far_copy(k, step).wait_recv()
        cut = pl.ds(pl.multiple_of(b * rows, rows), rows)
        weight = -(cond_in[:, cut, :].astype(jnp.int32).astype(jnp.float32) * (1.0 / COND_STEPS) + COND_MID)

        @pl.loop(0, readings // 8)
        def _(block):
            for n in range(8):
                m = block * 8 + n
                first, second, third, fourth = (spots[4 * m + c] for c in range(4))
                product = minus(own[b, first], own[b, second]) * minus(far[k][third], far[k][fourth])
                out[m, :, cut, :] = (weight * (product[0] + product[1] + product[2])).astype(jnp.bfloat16)

    def take_near(h):
        @pl.loop(0, half)
        def _(j):
            r = near0 + j

            @pl.when(r == me)
            def _():
                own_planes(h).wait()

            @pl.when(r != me)
            def _():
                plane_wait(h, 1, r)
                plane_wait(h, 2, r)

                @pl.when(me > 0)
                def _():
                    plane_wait(h, 0, r)

                @pl.when(me < slabs - 1)
                def _():
                    plane_wait(h, 3, r)

            @pl.loop(0, 4)
            def _(slot):
                decode_plane(h, r, slot)

    def take_far(h, slot):
        @pl.loop(0, half)
        def _(j):
            r = far0 + j
            plane_wait(h, slot, r)

            @pl.when(downs if slot == 1 else ups)
            def _():
                (forward_down if slot == 1 else forward_up)(h, r).start()

            decode_plane(h, r, slot)

    def take_edges(h):
        @pl.loop(0, half)
        def _(j):
            r = far0 + j

            @pl.when(me < slabs - 1)
            def _():
                plane_wait(h, 3, r)

            decode_plane(h, r, 3)

            @pl.when(me > 0)
            def _():
                plane_wait(h, 0, r)

            decode_plane(h, r, 0)

    inside = upper * (half + 1)
    beyond = (1 - upper) * (half - 1)
    both = (0, 1)

    def each(start, number, act):
        @pl.loop(0, number)
        def _(j):
            act(start + j)

    take_far(0, 1)
    take_near(0)
    each(inside, half - 1, lambda b: gradients(0, b, both, both))
    for k in range(half - 1):
        offer(k, inside + k)
    take_far(0, 2)
    send_near(1)
    take_edges(0)
    each(beyond, half + 1, lambda b: gradients(0, b, both, both))
    for k in range(half + 1):
        offer(half - 1 + k, beyond + k)
    take_far(1, 1)
    take_near(1)
    each(inside, half - 1, lambda b: gradients(1, b, both, both))
    each(beyond, half + 1, lambda b: gradients(1, b, (0,), ()))
    take_far(1, 2)
    for step in range(1, slabs):
        cond_copy(step).wait_recv()
    own_cond.wait()
    for k in range(half - 1):
        finish(k, inside + k)
    each(beyond, half + 1, lambda b: gradients(1, b, (1,), ()))
    take_edges(1)
    each(beyond, half + 1, lambda b: gradients(1, b, (), both))
    for k in range(half + 1):
        finish(half - 1 + k, beyond + k)

    @pl.loop(0, slabs)
    def _(d):
        for h in range(2):

            @pl.when(d != me)
            def _(h=h):
                plane_copy(h, 1, d).wait_send()
                plane_copy(h, 2, d).wait_send()
                edge_copies(h, d, lambda copy: copy.wait_send())

            @pl.when((d // half != upper) & ups)
            def _(h=h):
                forward_up(h, d).wait_send()

            @pl.when((d // half != upper) & downs)
            def _(h=h):
                forward_down(h, d).wait_send()

    for step in range(1, slabs):
        cond_copy(step).wait_send()
    for step in range(1, groups):
        ask_copy(step).wait_send()
    for k in range(slabs):
        for step in range(1, groups):
            far_copy(k, step).wait_send()


def exchange(potentials, conductivity, quadrupoles, slabs, groups):
    count, depth, rows, width = potentials.shape
    readings = quadrupoles.shape[0]
    x_size = rows * slabs
    anywhere = pl.BlockSpec(memory_space=pl.ANY)
    dma = pltpu.SemaphoreType.DMA
    bf16, f32, i16, i32 = jnp.bfloat16, jnp.float32, jnp.int16, jnp.int32
    asks = (groups - 1) * REQ
    return pl.pallas_call(
        functools.partial(exchange_kernel, slabs, groups),
        out_shape=pltpu.VMEM((readings, 2, x_size, width), bf16),
        in_specs=[anywhere, anywhere, pl.BlockSpec(memory_space=pltpu.VMEM), pl.BlockSpec(memory_space=pltpu.SMEM)],
        out_specs=pl.BlockSpec(memory_space=pltpu.VMEM),
        scratch_shapes=[
            pltpu.VMEM((count, depth, rows, width), f32),
            pltpu.VMEM((depth, rows, width), f32),
            pltpu.VMEM((slabs // 2, rows * count // 2, width), f32),
            pltpu.VMEM((depth + 2, 2, rows + 1, count // 2, width), i16),
            pltpu.VMEM((slabs, 4, 2, rows + 1, count // 2, width), i16),
            pltpu.VMEM((4 * count * (x_size + 16), width), f32),
            pltpu.VMEM((depth, rows, width), i16),
            pltpu.VMEM((2, x_size, width), i16),
            pltpu.VMEM((groups, 8, 128), i32),
            pltpu.SMEM((groups, 8, 128), i32),
            pltpu.VMEM((8, 128), i32),
            pltpu.SMEM((8, 128), i32),
            pltpu.VMEM((groups, 8, 128), i32),
            pltpu.SMEM((4 * readings,), i32),
            pltpu.VMEM((slabs, count, 3, 2, rows, width), bf16),
            pltpu.VMEM((slabs, groups - 1, REQ, 3, 2, rows, width), bf16),
        ]
        + [pltpu.VMEM((asks, 3, 2, rows, width), bf16)] * slabs
        + [
            dma((2, 4, slabs)),
            dma((2, 4, slabs)),
            dma((2, 2, slabs)),
            dma((slabs,)),
            dma((slabs,)),
            dma((groups,)),
            dma((groups,)),
            dma((slabs, groups)),
            dma((slabs, groups)),
            dma((PARTS,)),
            dma((6,)),
        ],
        compiler_params=pltpu.CompilerParams(
            collective_id=0, has_side_effects=True, vmem_limit_bytes=50 * 1024 * 1024
        ),
        name="exchange",
    )(potentials, conductivity, quadrupoles, quadrupoles.reshape(-1))


def deliver_kernel(source, target, done):
    share = source.shape[0] // PARTS
    copies = [
        pltpu.make_async_copy(source.at[pl.ds(k * share, share)], target.at[pl.ds(k * share, share)], done.at[k])
        for k in range(PARTS)
    ]
    for copy in copies:
        copy.start()
    for copy in copies:
        copy.wait()


def deliver(rows):
    return pl.pallas_call(
        deliver_kernel,
        out_shape=jax.ShapeDtypeStruct(rows.shape, rows.dtype),
        in_specs=[pl.BlockSpec(memory_space=pl.ANY)],
        out_specs=pl.BlockSpec(memory_space=pl.ANY),
        scratch_shapes=[pltpu.SemaphoreType.DMA((PARTS,))],
        compiler_params=pltpu.CompilerParams(vmem_limit_bytes=1024 * 1024),
        name="deliver",
    )(rows)


def general(potentials, conductivity, quadrupoles):
    shifted = lax.all_to_all(potentials, "slab", split_axis=1, concat_axis=2, tiled=True)
    cond = lax.all_to_all(conductivity[None], "slab", split_axis=1, concat_axis=2, tiled=True)[0]
    slabs = lax.axis_size("slab")
    ends = slabs - 1
    last = shifted.shape[1] - 1
    below = lax.ppermute(shifted[:, last:], "slab", [(i, i + 1) for i in range(ends)])
    above = lax.ppermute(shifted[:, :1], "slab", [(i + 1, i) for i in range(ends)])
    tall = jnp.concatenate([below, shifted, above], axis=1)
    wide = jnp.pad(shifted, ((0, 0), (0, 0), (1, 1), (1, 1)))
    grads = jnp.stack(
        [
            (tall[:, 2:] - tall[:, :-2]) * 0.5,
            (wide[:, :, 2:, 1:-1] - wide[:, :, :-2, 1:-1]) * 0.5,
            (wide[:, :, 1:-1, 2:] - wide[:, :, 1:-1, :-2]) * 0.5,
        ],
        1,
    ).astype(jnp.bfloat16)
    table = lax.all_gather(grads.reshape(grads.shape[0], 3, -1), "elec", axis=0, tiled=True)
    ids = jnp.arange(table.shape[0], dtype=jnp.int32)
    hot = (quadrupoles[:, :, None] == ids).astype(jnp.bfloat16)
    flat = table.reshape(table.shape[0], -1)
    shape = (quadrupoles.shape[0], 3, -1)
    source = jnp.dot(hot[:, 0] - hot[:, 1], flat, preferred_element_type=jnp.float32).reshape(shape)
    probe = jnp.dot(hot[:, 2] - hot[:, 3], flat, preferred_element_type=jnp.float32).reshape(shape)
    rows = -(cond.reshape(-1)[None] * jnp.sum(source * probe, axis=1))
    return rows.astype(jnp.bfloat16).reshape((quadrupoles.shape[0],) + shifted.shape[1:])


def shards(potentials, conductivity, quadrupoles):
    slabs, groups = lax.axis_size("slab"), lax.axis_size("elec")
    count, depth, rows, width = potentials.shape
    fits = rows == 16 and width == 128 and depth == 2 * slabs and slabs % 4 == 0
    if not fits or count % 32 or 2 * (groups - 1) * REQ > count or count * groups != width or quadrupoles.shape[0] % 8:
        return general(potentials, conductivity, quadrupoles)
    return deliver(exchange(potentials, conductivity, quadrupoles, slabs, groups))


def solution(mesh):
    in_specs = (P("elec", None, "slab", None), P(None, "slab", None), P("elec", None))
    out_specs = P("elec", "slab", None, None)
    return jax.shard_map(shards, mesh=mesh, in_specs=in_specs, out_specs=out_specs, check_vma=False)
```

```python
import functools

import jax
import jax.numpy as jnp
from jax import lax
from jax.experimental import pallas as pl
from jax.experimental.pallas import tpu as pltpu
from jax.sharding import PartitionSpec as P

MESH = pl.DeviceIdType.MESH
REQ = 4
PARTS = 4
SPAN = 12.5
LEVELS = 32767.0
GROUP = 8
COND_MID = 0.55
COND_STEPS = 32766.0 / 0.45


def minus(first, second):
    return (first - second).astype(jnp.float32)


def decode(code):
    root = code.astype(jnp.int32).astype(jnp.float32) * (SPAN**0.125 / LEVELS)
    square = root * root
    fourth = square * square
    return (root * jnp.abs(root)) * square * fourth


def encode(step):
    level = jnp.exp2(jnp.log2(jnp.abs(step) * (1.0 / SPAN)) * 0.125) * LEVELS
    level = (level + 0.5).astype(jnp.int32)
    return jnp.where(step < 0, -level, level).astype(jnp.int16)


def exchange_kernel(slabs, groups, *refs):
    pot, cond, quads, index, out = refs[:5]
    pot_v, cond_v, stage, enc, cin, field, cond_code, cond_in = refs[5:13]
    asked_in, asked_s, place_v, place_s, asked, spots, own, box = refs[13:21]
    far = refs[21 : 21 + slabs]
    plane_send, plane_recv, fwd_send, cond_send, cond_recv = refs[21 + slabs : 26 + slabs]
    ask_send, ask_recv, far_send, far_recv, pot_sem, local = refs[26 + slabs :]

    count, depth, rows, width = pot.shape
    slots = rows + 1
    some = count // 2
    half = slabs // 2
    x_size = rows * slabs
    tall = x_size + 16
    readings = out.shape[0]
    me = lax.axis_index("slab")
    group = lax.axis_index("elec")
    upper = me // half
    near0 = upper * half
    far0 = (1 - upper) * half
    my_rows = pl.ds(pl.multiple_of(me * rows, rows), rows)

    share = count // PARTS
    loads = [
        pltpu.make_async_copy(pot.at[pl.ds(k * share, share)], pot_v.at[pl.ds(k * share, share)], pot_sem.at[k])
        for k in range(PARTS)
    ]
    cond_load = pltpu.make_async_copy(cond, cond_v, local.at[0])

    barrier = pltpu.get_barrier_semaphore()
    for step in range(1, groups):
        pl.semaphore_signal(barrier, inc=1, device_id={"elec": lax.rem(group + step, groups)}, device_id_type=MESH)
    for step in range(1, slabs):
        pl.semaphore_signal(barrier, inc=1, device_id={"slab": lax.rem(me + step, slabs)}, device_id_type=MESH)
    for copy in loads:
        copy.start()
    cond_load.start()

    blank = jnp.zeros((2, slots, some, width), jnp.int16)
    enc[0] = blank
    enc[depth + 1] = blank

    @pl.when(me == 0)
    def _():
        @pl.loop(1, slabs)
        def _(r):
            cin[r, 0] = blank

    @pl.when(me == slabs - 1)
    def _():
        @pl.loop(0, slabs - 1)
        def _(r):
            cin[r, 3] = blank

    @pl.loop(0, 2 * count)
    def _(k):
        base = (count + k) * tall
        edge = jnp.zeros((8, width), jnp.float32)
        field[pl.ds(pl.multiple_of(base, 8), 8), :] = edge
        field[pl.ds(pl.multiple_of(base + tall - 8, 8), 8), :] = edge

    lane = lax.broadcasted_iota(jnp.int32, (width, width), 1)
    down_id = lax.broadcasted_iota(jnp.int32, (width, width), 0)

    def turned(flat):
        return jnp.broadcast_to(jnp.sum(jnp.where(down_id == lane, flat, 0), axis=1, keepdims=True), (width, width))

    ids = lax.broadcasted_iota(jnp.int32, (readings, width), 1)
    third, fourth = (jnp.broadcast_to(quads[:, c : c + 1], (readings, width)) for c in (2, 3))
    named = jnp.sum(jnp.where((third == ids) | (fourth == ids), 1, 0), axis=0, keepdims=True)
    named = turned(jnp.broadcast_to(jnp.minimum(named, 1), (width, width)))
    earlier = (lane // count == down_id // count) & (down_id < lane)
    rank = jnp.sum(jnp.where(earlier, named, 0), axis=0, keepdims=True)
    across = lane[0:1]
    away = lax.rem(across // count - group + groups, groups)
    spot = jnp.where(away == 0, 0, (away - 1) * REQ + jnp.minimum(rank, REQ - 1))
    rank_down = turned(jnp.broadcast_to(rank, (width, width)))
    away_down = lax.rem(down_id // count - group + groups, groups)
    for step in range(1, groups):
        hit = (named > 0) & (away_down == step) & (rank_down == lane)
        chosen = jnp.sum(jnp.where(hit, lax.rem(down_id, count), 0), axis=0, keepdims=True)
        asked[step] = jnp.broadcast_to(chosen, (8, width))

    pl.semaphore_wait(barrier, slabs + groups - 2)

    def ask_copy(step):
        return pltpu.make_async_remote_copy(
            src_ref=asked.at[step],
            dst_ref=asked_in.at[step],
            send_sem=ask_send.at[step],
            recv_sem=ask_recv.at[step],
            device_id={"elec": lax.rem(group + step, groups)},
            device_id_type=MESH,
        )

    for step in range(1, groups):
        ask_copy(step).start()

    def plane_copy(h, slot, d):
        return pltpu.make_async_remote_copy(
            src_ref=enc.at[2 * d + slot, h],
            dst_ref=cin.at[me, slot, h],
            send_sem=plane_send.at[h, slot, d],
            recv_sem=plane_recv.at[h, slot, me],
            device_id={"slab": d},
            device_id_type=MESH,
        )

    def plane_wait(h, slot, r):
        pltpu.make_async_remote_copy(
            src_ref=enc.at[slot, h],
            dst_ref=cin.at[r, slot, h],
            send_sem=plane_send.at[h, slot, r],
            recv_sem=plane_recv.at[h, slot, r],
            device_id={"slab": r},
            device_id_type=MESH,
        ).wait_recv()

    def forward_up(h, r):
        return pltpu.make_async_remote_copy(
            src_ref=cin.at[r, 2, h],
            dst_ref=cin.at[r, 0, h],
            send_sem=fwd_send.at[h, 0, r],
            recv_sem=plane_recv.at[h, 0, r],
            device_id={"slab": lax.rem(me + 1, slabs)},
            device_id_type=MESH,
        )

    def forward_down(h, r):
        return pltpu.make_async_remote_copy(
            src_ref=cin.at[r, 1, h],
            dst_ref=cin.at[r, 3, h],
            send_sem=fwd_send.at[h, 1, r],
            recv_sem=plane_recv.at[h, 3, r],
            device_id={"slab": lax.rem(me + slabs - 1, slabs)},
            device_id_type=MESH,
        )

    ups = (me != slabs - 1) & (me != half - 1)
    downs = (me != 0) & (me != half)

    def cond_copy(step):
        to = lax.rem(me + step, slabs)
        return pltpu.make_async_remote_copy(
            src_ref=cond_code.at[pl.ds(to * 2, 2)],
            dst_ref=cond_in.at[:, my_rows, :],
            send_sem=cond_send.at[step],
            recv_sem=cond_recv.at[step],
            device_id={"slab": to},
            device_id_type=MESH,
        )

    own_cond = pltpu.make_async_copy(cond_code.at[pl.ds(me * 2, 2)], cond_in.at[:, my_rows, :], local.at[1])

    def own_planes(h):
        return pltpu.make_async_copy(enc.at[pl.ds(2 * me, 4), h], cin.at[me, :, h], local.at[4 + h])

    cond_load.wait()

    @pl.loop(0, depth)
    def _(z):
        level = (cond_v[z] - COND_MID) * COND_STEPS
        level = level + jnp.where(level < 0, -0.5, 0.5)
        cond_code[z] = level.astype(jnp.int32).astype(jnp.int16)

    for step in range(1, slabs):
        cond_copy(step).start()
    own_cond.start()

    for step in range(1, groups):
        ask_copy(step).wait_recv()
    asked_copy = pltpu.make_async_copy(asked_in, asked_s, local.at[2])
    asked_copy.start()

    e_row = lax.broadcasted_iota(jnp.int32, (count, width), 0)
    lane = lax.broadcasted_iota(jnp.int32, (count, width), 1)
    hits = jnp.zeros((count, width), jnp.int32)
    for step in range(1, groups):
        wanted = jnp.broadcast_to(asked_in[step, 0:1, :], (count, width))
        hits = hits + jnp.where((wanted == e_row) & (lane < REQ), 1, 0)
    mark = jnp.broadcast_to(jnp.minimum(jnp.sum(hits, axis=1, keepdims=True), 1), (count, width))
    total = jnp.sum(mark, axis=0, keepdims=True)
    before = jnp.sum(jnp.where(e_row < lane, mark, 0), axis=0, keepdims=True)
    here = jnp.sum(jnp.where(e_row == lane, mark, 0), axis=0, keepdims=True)
    place = jnp.where(here > 0, before, total + lane[0:1] - before)
    across = jnp.broadcast_to(place, (count, width))
    down = jnp.sum(jnp.where(e_row == lane, across, 0), axis=1, keepdims=True)
    order = jnp.sum(jnp.where(jnp.broadcast_to(down, (count, width)) == lane, e_row, 0), axis=0, keepdims=True)
    eight = lax.broadcasted_iota(jnp.int32, (8, width), 0)
    table = jnp.where(eight == 0, jnp.broadcast_to(place, (8, width)), jnp.broadcast_to(order, (8, width)))
    place_v[...] = jnp.where(eight == 2, jnp.broadcast_to(spot, (8, width)), table)
    place_copy = pltpu.make_async_copy(place_v, place_s, local.at[3])
    place_copy.start()
    asked_copy.wait()
    place_copy.wait()
    for copy in loads:
        copy.wait()

    def edge_copies(h, d, act):
        close = d // half == upper

        @pl.when((d > 0) & (close | (d == half)))
        def _():
            act(plane_copy(h, 0, d))

        @pl.when((d < slabs - 1) & (close | (d == half - 1)))
        def _():
            act(plane_copy(h, 3, d))

    facing = jnp.where(upper == 0, half, half - 1)

    def send_near(h):
        own_planes(h).start()

        @pl.loop(0, half)
        def _(q):
            @pl.when(near0 + q != me)
            def _():
                plane_copy(h, 1, near0 + q).start()
                plane_copy(h, 2, near0 + q).start()

        @pl.loop(0, half)
        def _(q):
            @pl.when(near0 + q != me)
            def _():
                edge_copies(h, near0 + q, lambda copy: copy.start())

    @pl.loop(0, 8)
    def _(n):
        h, kind = n // 4, lax.rem(n, 4)
        d0 = jnp.where(kind < 2, far0, near0)
        z0 = 2 * d0 + lax.rem(kind, 2)

        @pl.loop(0, some)
        def _(j):
            e = place_s[1, h * some + j]
            for q in range(half):
                stage[q, pl.ds(j, rows, stride=some), :] = pot_v[e, z0 + 2 * q]

        reached = [jnp.zeros((some, width), jnp.float32)] * half
        for slot in range(slots):
            for q in range(half):
                code = encode(stage[q, pl.ds(max(slot - 1, 0) * some, some), :] - reached[q])
                enc[z0 + 2 * q + 1, h, slot] = code
                reached[q] = reached[q] + decode(code)

        @pl.when(kind < 2)
        def _():
            @pl.loop(0, half)
            def _(q):
                plane_copy(h, 1 + kind, far0 + q).start()

        @pl.when(kind == 3)
        def _():
            edge_copies(h, facing, lambda copy: copy.start())

        @pl.when(n == 3)
        def _():
            send_near(0)

    @pl.loop(0, readings // 4)
    def _(block):
        for n in range(4):
            m = block * 4 + n
            for c in range(2):
                spots[4 * m + c] = place_s[0, lax.rem(index[4 * m + c], count)]
                spots[4 * m + 2 + c] = place_s[2, index[4 * m + 2 + c]]

    def decode_plane(h, r, slot):
        reached = jnp.zeros((some, width), jnp.float32)
        for k in range(slots):
            reached = reached + decode(cin[r, slot, h, k])
            if k > 0:
                start = (slot * count + h * some) * tall + 8 + r * rows + k - 1
                field[pl.ds(start, some, stride=tall), :] = reached

    row_lane = lax.broadcasted_iota(jnp.int32, (rows, width), 1)

    def gradients(h, b, flat, steep):
        @pl.loop(0, some // GROUP)
        def _(n):
            for e in [h * some + n * GROUP + g for g in range(GROUP)]:

                def at(slot, shift, e=e):
                    return field[pl.ds((slot * count + e) * tall + 8 + b * rows + shift, rows), :]

                for i in steep:
                    own[b, e, 0, i] = ((at(2 + i, 0) - at(i, 0)) * 0.5).astype(jnp.bfloat16)
                for i in flat:
                    here = at(1 + i, 0)
                    right = jnp.where(row_lane < width - 1, pltpu.roll(here, width - 1, 1), 0.0)
                    left = jnp.where(row_lane > 0, pltpu.roll(here, 1, 1), 0.0)
                    own[b, e, 1, i] = ((at(1 + i, 1) - at(1 + i, -1)) * 0.5).astype(jnp.bfloat16)
                    own[b, e, 2, i] = ((right - left) * 0.5).astype(jnp.bfloat16)

    def far_copy(k, step):
        return pltpu.make_async_remote_copy(
            src_ref=box.at[k, step - 1],
            dst_ref=far[k].at[pl.ds((groups - 1 - step) * REQ, REQ)],
            send_sem=far_send.at[k, step],
            recv_sem=far_recv.at[k, step],
            device_id={"elec": lax.rem(group + step, groups)},
            device_id_type=MESH,
        )

    def offer(k, b):
        for step in range(1, groups):
            for which in range(REQ):
                chosen = place_s[0, asked_s[groups - step, 0, which]]
                box[k, step - 1, which] = own[b, chosen]
            far_copy(k, step).start()

    def finish(k, b):
        for step in range(1, groups):
            far_copy(k, step).wait_recv()
        cut = pl.ds(pl.multiple_of(b * rows, rows), rows)
        weight = -(cond_in[:, cut, :].astype(jnp.int32).astype(jnp.float32) * (1.0 / COND_STEPS) + COND_MID)

        @pl.loop(0, readings // 8)
        def _(block):
            for n in range(8):
                m = block * 8 + n
                first, second, third, fourth = (spots[4 * m + c] for c in range(4))
                product = minus(own[b, first], own[b, second]) * minus(far[k][third], far[k][fourth])
                out[m, :, cut, :] = (weight * (product[0] + product[1] + product[2])).astype(jnp.bfloat16)

    def take_near(h):
        @pl.loop(0, half)
        def _(j):
            r = near0 + j

            @pl.when(r == me)
            def _():
                own_planes(h).wait()

            @pl.when(r != me)
            def _():
                plane_wait(h, 1, r)
                plane_wait(h, 2, r)

                @pl.when(me > 0)
                def _():
                    plane_wait(h, 0, r)

                @pl.when(me < slabs - 1)
                def _():
                    plane_wait(h, 3, r)

            @pl.loop(0, 4)
            def _(slot):
                decode_plane(h, r, slot)

    def take_far(h, slot):
        @pl.loop(0, half)
        def _(j):
            r = far0 + j
            plane_wait(h, slot, r)

            @pl.when(downs if slot == 1 else ups)
            def _():
                (forward_down if slot == 1 else forward_up)(h, r).start()

            decode_plane(h, r, slot)

    def take_edges(h):
        @pl.loop(0, half)
        def _(j):
            r = far0 + j

            @pl.when(me < slabs - 1)
            def _():
                plane_wait(h, 3, r)

            decode_plane(h, r, 3)

            @pl.when(me > 0)
            def _():
                plane_wait(h, 0, r)

            decode_plane(h, r, 0)

    inside = upper * (half + 1)
    beyond = (1 - upper) * (half - 1)
    both = (0, 1)

    def each(start, number, act):
        @pl.loop(0, number)
        def _(j):
            act(start + j)

    take_far(0, 1)
    take_near(0)
    each(inside, half - 1, lambda b: gradients(0, b, both, both))
    for k in range(half - 1):
        offer(k, inside + k)
    take_far(0, 2)
    send_near(1)
    take_edges(0)
    each(beyond, half + 1, lambda b: gradients(0, b, both, both))
    for k in range(half + 1):
        offer(half - 1 + k, beyond + k)
    take_far(1, 1)
    take_near(1)
    each(inside, half - 1, lambda b: gradients(1, b, both, both))
    each(beyond, half + 1, lambda b: gradients(1, b, (0,), ()))
    take_far(1, 2)
    for step in range(1, slabs):
        cond_copy(step).wait_recv()
    own_cond.wait()
    for k in range(half - 1):
        finish(k, inside + k)
    each(beyond, half + 1, lambda b: gradients(1, b, (1,), ()))
    take_edges(1)
    each(beyond, half + 1, lambda b: gradients(1, b, (), both))
    for k in range(half + 1):
        finish(half - 1 + k, beyond + k)

    @pl.loop(0, slabs)
    def _(d):
        for h in range(2):

            @pl.when(d != me)
            def _(h=h):
                plane_copy(h, 1, d).wait_send()
                plane_copy(h, 2, d).wait_send()
                edge_copies(h, d, lambda copy: copy.wait_send())

            @pl.when((d // half != upper) & ups)
            def _(h=h):
                forward_up(h, d).wait_send()

            @pl.when((d // half != upper) & downs)
            def _(h=h):
                forward_down(h, d).wait_send()

    for step in range(1, slabs):
        cond_copy(step).wait_send()
    for step in range(1, groups):
        ask_copy(step).wait_send()
    for k in range(slabs):
        for step in range(1, groups):
            far_copy(k, step).wait_send()


def exchange(potentials, conductivity, quadrupoles, slabs, groups):
    count, depth, rows, width = potentials.shape
    readings = quadrupoles.shape[0]
    x_size = rows * slabs
    anywhere = pl.BlockSpec(memory_space=pl.ANY)
    dma = pltpu.SemaphoreType.DMA
    bf16, f32, i16, i32 = jnp.bfloat16, jnp.float32, jnp.int16, jnp.int32
    asks = (groups - 1) * REQ
    return pl.pallas_call(
        functools.partial(exchange_kernel, slabs, groups),
        out_shape=pltpu.VMEM((readings, 2, x_size, width), bf16),
        in_specs=[anywhere, anywhere, pl.BlockSpec(memory_space=pltpu.VMEM), pl.BlockSpec(memory_space=pltpu.SMEM)],
        out_specs=pl.BlockSpec(memory_space=pltpu.VMEM),
        scratch_shapes=[
            pltpu.VMEM((count, depth, rows, width), f32),
            pltpu.VMEM((depth, rows, width), f32),
            pltpu.VMEM((slabs // 2, rows * count // 2, width), f32),
            pltpu.VMEM((depth + 2, 2, rows + 1, count // 2, width), i16),
            pltpu.VMEM((slabs, 4, 2, rows + 1, count // 2, width), i16),
            pltpu.VMEM((4 * count * (x_size + 16), width), f32),
            pltpu.VMEM((depth, rows, width), i16),
            pltpu.VMEM((2, x_size, width), i16),
            pltpu.VMEM((groups, 8, 128), i32),
            pltpu.SMEM((groups, 8, 128), i32),
            pltpu.VMEM((8, 128), i32),
            pltpu.SMEM((8, 128), i32),
            pltpu.VMEM((groups, 8, 128), i32),
            pltpu.SMEM((4 * readings,), i32),
            pltpu.VMEM((slabs, count, 3, 2, rows, width), bf16),
            pltpu.VMEM((slabs, groups - 1, REQ, 3, 2, rows, width), bf16),
        ]
        + [pltpu.VMEM((asks, 3, 2, rows, width), bf16)] * slabs
        + [
            dma((2, 4, slabs)),
            dma((2, 4, slabs)),
            dma((2, 2, slabs)),
            dma((slabs,)),
            dma((slabs,)),
            dma((groups,)),
            dma((groups,)),
            dma((slabs, groups)),
            dma((slabs, groups)),
            dma((PARTS,)),
            dma((6,)),
        ],
        compiler_params=pltpu.CompilerParams(
            collective_id=0, has_side_effects=True, vmem_limit_bytes=50 * 1024 * 1024
        ),
        name="exchange",
    )(potentials, conductivity, quadrupoles, quadrupoles.reshape(-1))


def deliver_kernel(source, target, done):
    share = source.shape[0] // PARTS
    copies = [
        pltpu.make_async_copy(source.at[pl.ds(k * share, share)], target.at[pl.ds(k * share, share)], done.at[k])
        for k in range(PARTS)
    ]
    for copy in copies:
        copy.start()
    for copy in copies:
        copy.wait()


def deliver(rows):
    return pl.pallas_call(
        deliver_kernel,
        out_shape=jax.ShapeDtypeStruct(rows.shape, rows.dtype),
        in_specs=[pl.BlockSpec(memory_space=pl.ANY)],
        out_specs=pl.BlockSpec(memory_space=pl.ANY),
        scratch_shapes=[pltpu.SemaphoreType.DMA((PARTS,))],
        compiler_params=pltpu.CompilerParams(vmem_limit_bytes=1024 * 1024),
        name="deliver",
    )(rows)


def general(potentials, conductivity, quadrupoles):
    shifted = lax.all_to_all(potentials, "slab", split_axis=1, concat_axis=2, tiled=True)
    cond = lax.all_to_all(conductivity[None], "slab", split_axis=1, concat_axis=2, tiled=True)[0]
    slabs = lax.axis_size("slab")
    ends = slabs - 1
    last = shifted.shape[1] - 1
    below = lax.ppermute(shifted[:, last:], "slab", [(i, i + 1) for i in range(ends)])
    above = lax.ppermute(shifted[:, :1], "slab", [(i + 1, i) for i in range(ends)])
    tall = jnp.concatenate([below, shifted, above], axis=1)
    wide = jnp.pad(shifted, ((0, 0), (0, 0), (1, 1), (1, 1)))
    grads = jnp.stack(
        [
            (tall[:, 2:] - tall[:, :-2]) * 0.5,
            (wide[:, :, 2:, 1:-1] - wide[:, :, :-2, 1:-1]) * 0.5,
            (wide[:, :, 1:-1, 2:] - wide[:, :, 1:-1, :-2]) * 0.5,
        ],
        1,
    ).astype(jnp.bfloat16)
    table = lax.all_gather(grads.reshape(grads.shape[0], 3, -1), "elec", axis=0, tiled=True)
    ids = jnp.arange(table.shape[0], dtype=jnp.int32)
    hot = (quadrupoles[:, :, None] == ids).astype(jnp.bfloat16)
    flat = table.reshape(table.shape[0], -1)
    shape = (quadrupoles.shape[0], 3, -1)
    source = jnp.dot(hot[:, 0] - hot[:, 1], flat, preferred_element_type=jnp.float32).reshape(shape)
    probe = jnp.dot(hot[:, 2] - hot[:, 3], flat, preferred_element_type=jnp.float32).reshape(shape)
    rows = -(cond.reshape(-1)[None] * jnp.sum(source * probe, axis=1))
    return rows.astype(jnp.bfloat16).reshape((quadrupoles.shape[0],) + shifted.shape[1:])


def shards(potentials, conductivity, quadrupoles):
    slabs, groups = lax.axis_size("slab"), lax.axis_size("elec")
    count, depth, rows, width = potentials.shape
    fits = rows == 16 and width == 128 and depth == 2 * slabs and slabs % 4 == 0
    if not fits or count % 32 or 2 * (groups - 1) * REQ > count or count * groups != width or quadrupoles.shape[0] % 8:
        return general(potentials, conductivity, quadrupoles)
    return deliver(exchange(potentials, conductivity, quadrupoles, slabs, groups))


def solution(mesh):
    in_specs = (P("elec", None, "slab", None), P(None, "slab", None), P("elec", None))
    out_specs = P("elec", "slab", None, None)
    return jax.shard_map(shards, mesh=mesh, in_specs=in_specs, out_specs=out_specs, check_vma=False)
```

```python
import functools

import jax
import jax.numpy as jnp
from jax import lax
from jax.experimental import pallas as pl
from jax.experimental.pallas import tpu as pltpu
from jax.sharding import PartitionSpec as P

MESH = pl.DeviceIdType.MESH
REQ = 4
PARTS = 4
SPAN = 12.5
LEVELS = 32767.0
GROUP = 16
COND_MID = 0.55
COND_STEPS = 32766.0 / 0.45


def minus(first, second):
    return (first - second).astype(jnp.float32)


def decode(code):
    root = code.astype(jnp.int32).astype(jnp.float32) * (SPAN**0.125 / LEVELS)
    square = root * root
    fourth = square * square
    return (root * jnp.abs(root)) * square * fourth


def encode(step):
    level = jnp.exp2(jnp.log2(jnp.abs(step) * (1.0 / SPAN)) * 0.125) * LEVELS
    level = (level + 0.5).astype(jnp.int32)
    return jnp.where(step < 0, -level, level).astype(jnp.int16)


def exchange_kernel(slabs, groups, *refs):
    pot, cond, quads, index, out = refs[:5]
    pot_v, cond_v, stage, enc, cin, field, cond_code, cond_in = refs[5:13]
    asked_in, asked_s, place_v, place_s, asked, spots, own, box = refs[13:21]
    far = refs[21 : 21 + slabs]
    plane_send, plane_recv, fwd_send, cond_send, cond_recv = refs[21 + slabs : 26 + slabs]
    ask_send, ask_recv, far_send, far_recv, pot_sem, local = refs[26 + slabs :]

    count, depth, rows, width = pot.shape
    slots = rows + 1
    some = count // 2
    half = slabs // 2
    x_size = rows * slabs
    tall = x_size + 16
    readings = out.shape[0]
    me = lax.axis_index("slab")
    group = lax.axis_index("elec")
    upper = me // half
    near0 = upper * half
    far0 = (1 - upper) * half
    my_rows = pl.ds(pl.multiple_of(me * rows, rows), rows)

    share = count // PARTS
    loads = [
        pltpu.make_async_copy(pot.at[pl.ds(k * share, share)], pot_v.at[pl.ds(k * share, share)], pot_sem.at[k])
        for k in range(PARTS)
    ]
    cond_load = pltpu.make_async_copy(cond, cond_v, local.at[0])

    barrier = pltpu.get_barrier_semaphore()
    for step in range(1, groups):
        pl.semaphore_signal(barrier, inc=1, device_id={"elec": lax.rem(group + step, groups)}, device_id_type=MESH)
    for step in range(1, slabs):
        pl.semaphore_signal(barrier, inc=1, device_id={"slab": lax.rem(me + step, slabs)}, device_id_type=MESH)
    for copy in loads:
        copy.start()
    cond_load.start()

    blank = jnp.zeros((2, slots, some, width), jnp.int16)
    enc[0] = blank
    enc[depth + 1] = blank

    @pl.when(me == 0)
    def _():
        @pl.loop(1, slabs)
        def _(r):
            cin[r, 0] = blank

    @pl.when(me == slabs - 1)
    def _():
        @pl.loop(0, slabs - 1)
        def _(r):
            cin[r, 3] = blank

    @pl.loop(0, 2 * count)
    def _(k):
        base = (count + k) * tall
        edge = jnp.zeros((8, width), jnp.float32)
        field[pl.ds(pl.multiple_of(base, 8), 8), :] = edge
        field[pl.ds(pl.multiple_of(base + tall - 8, 8), 8), :] = edge

    lane = lax.broadcasted_iota(jnp.int32, (width, width), 1)
    down_id = lax.broadcasted_iota(jnp.int32, (width, width), 0)

    def turned(flat):
        return jnp.broadcast_to(jnp.sum(jnp.where(down_id == lane, flat, 0), axis=1, keepdims=True), (width, width))

    ids = lax.broadcasted_iota(jnp.int32, (readings, width), 1)
    third, fourth = (jnp.broadcast_to(quads[:, c : c + 1], (readings, width)) for c in (2, 3))
    named = jnp.sum(jnp.where((third == ids) | (fourth == ids), 1, 0), axis=0, keepdims=True)
    named = turned(jnp.broadcast_to(jnp.minimum(named, 1), (width, width)))
    earlier = (lane // count == down_id // count) & (down_id < lane)
    rank = jnp.sum(jnp.where(earlier, named, 0), axis=0, keepdims=True)
    across = lane[0:1]
    away = lax.rem(across // count - group + groups, groups)
    spot = jnp.where(away == 0, 0, (away - 1) * REQ + jnp.minimum(rank, REQ - 1))
    rank_down = turned(jnp.broadcast_to(rank, (width, width)))
    away_down = lax.rem(down_id // count - group + groups, groups)
    for step in range(1, groups):
        hit = (named > 0) & (away_down == step) & (rank_down == lane)
        chosen = jnp.sum(jnp.where(hit, lax.rem(down_id, count), 0), axis=0, keepdims=True)
        asked[step] = jnp.broadcast_to(chosen, (8, width))

    pl.semaphore_wait(barrier, slabs + groups - 2)

    def ask_copy(step):
        return pltpu.make_async_remote_copy(
            src_ref=asked.at[step],
            dst_ref=asked_in.at[step],
            send_sem=ask_send.at[step],
            recv_sem=ask_recv.at[step],
            device_id={"elec": lax.rem(group + step, groups)},
            device_id_type=MESH,
        )

    for step in range(1, groups):
        ask_copy(step).start()

    def plane_copy(h, slot, d):
        return pltpu.make_async_remote_copy(
            src_ref=enc.at[2 * d + slot, h],
            dst_ref=cin.at[me, slot, h],
            send_sem=plane_send.at[h, slot, d],
            recv_sem=plane_recv.at[h, slot, me],
            device_id={"slab": d},
            device_id_type=MESH,
        )

    def plane_wait(h, slot, r):
        pltpu.make_async_remote_copy(
            src_ref=enc.at[slot, h],
            dst_ref=cin.at[r, slot, h],
            send_sem=plane_send.at[h, slot, r],
            recv_sem=plane_recv.at[h, slot, r],
            device_id={"slab": r},
            device_id_type=MESH,
        ).wait_recv()

    def forward_up(h, r):
        return pltpu.make_async_remote_copy(
            src_ref=cin.at[r, 2, h],
            dst_ref=cin.at[r, 0, h],
            send_sem=fwd_send.at[h, 0, r],
            recv_sem=plane_recv.at[h, 0, r],
            device_id={"slab": lax.rem(me + 1, slabs)},
            device_id_type=MESH,
        )

    def forward_down(h, r):
        return pltpu.make_async_remote_copy(
            src_ref=cin.at[r, 1, h],
            dst_ref=cin.at[r, 3, h],
            send_sem=fwd_send.at[h, 1, r],
            recv_sem=plane_recv.at[h, 3, r],
            device_id={"slab": lax.rem(me + slabs - 1, slabs)},
            device_id_type=MESH,
        )

    ups = (me != slabs - 1) & (me != half - 1)
    downs = (me != 0) & (me != half)

    def cond_copy(step):
        to = lax.rem(me + step, slabs)
        return pltpu.make_async_remote_copy(
            src_ref=cond_code.at[pl.ds(to * 2, 2)],
            dst_ref=cond_in.at[:, my_rows, :],
            send_sem=cond_send.at[step],
            recv_sem=cond_recv.at[step],
            device_id={"slab": to},
            device_id_type=MESH,
        )

    own_cond = pltpu.make_async_copy(cond_code.at[pl.ds(me * 2, 2)], cond_in.at[:, my_rows, :], local.at[1])

    def own_planes(h):
        return pltpu.make_async_copy(enc.at[pl.ds(2 * me, 4), h], cin.at[me, :, h], local.at[4 + h])

    cond_load.wait()

    @pl.loop(0, depth)
    def _(z):
        level = (cond_v[z] - COND_MID) * COND_STEPS
        level = level + jnp.where(level < 0, -0.5, 0.5)
        cond_code[z] = level.astype(jnp.int32).astype(jnp.int16)

    for step in range(1, slabs):
        cond_copy(step).start()
    own_cond.start()

    for step in range(1, groups):
        ask_copy(step).wait_recv()
    asked_copy = pltpu.make_async_copy(asked_in, asked_s, local.at[2])
    asked_copy.start()

    e_row = lax.broadcasted_iota(jnp.int32, (count, width), 0)
    lane = lax.broadcasted_iota(jnp.int32, (count, width), 1)
    hits = jnp.zeros((count, width), jnp.int32)
    for step in range(1, groups):
        wanted = jnp.broadcast_to(asked_in[step, 0:1, :], (count, width))
        hits = hits + jnp.where((wanted == e_row) & (lane < REQ), 1, 0)
    mark = jnp.broadcast_to(jnp.minimum(jnp.sum(hits, axis=1, keepdims=True), 1), (count, width))
    total = jnp.sum(mark, axis=0, keepdims=True)
    before = jnp.sum(jnp.where(e_row < lane, mark, 0), axis=0, keepdims=True)
    here = jnp.sum(jnp.where(e_row == lane, mark, 0), axis=0, keepdims=True)
    place = jnp.where(here > 0, before, total + lane[0:1] - before)
    across = jnp.broadcast_to(place, (count, width))
    down = jnp.sum(jnp.where(e_row == lane, across, 0), axis=1, keepdims=True)
    order = jnp.sum(jnp.where(jnp.broadcast_to(down, (count, width)) == lane, e_row, 0), axis=0, keepdims=True)
    eight = lax.broadcasted_iota(jnp.int32, (8, width), 0)
    table = jnp.where(eight == 0, jnp.broadcast_to(place, (8, width)), jnp.broadcast_to(order, (8, width)))
    place_v[...] = jnp.where(eight == 2, jnp.broadcast_to(spot, (8, width)), table)
    place_copy = pltpu.make_async_copy(place_v, place_s, local.at[3])
    place_copy.start()
    asked_copy.wait()
    place_copy.wait()
    for copy in loads:
        copy.wait()

    def edge_copies(h, d, act):
        close = d // half == upper

        @pl.when((d > 0) & (close | (d == half)))
        def _():
            act(plane_copy(h, 0, d))

        @pl.when((d < slabs - 1) & (close | (d == half - 1)))
        def _():
            act(plane_copy(h, 3, d))

    facing = jnp.where(upper == 0, half, half - 1)

    def send_near(h):
        own_planes(h).start()

        @pl.loop(0, half)
        def _(q):
            @pl.when(near0 + q != me)
            def _():
                plane_copy(h, 1, near0 + q).start()
                plane_copy(h, 2, near0 + q).start()

        @pl.loop(0, half)
        def _(q):
            @pl.when(near0 + q != me)
            def _():
                edge_copies(h, near0 + q, lambda copy: copy.start())

    @pl.loop(0, 8)
    def _(n):
        h, kind = n // 4, lax.rem(n, 4)
        d0 = jnp.where(kind < 2, far0, near0)
        z0 = 2 * d0 + lax.rem(kind, 2)

        @pl.loop(0, some)
        def _(j):
            e = place_s[1, h * some + j]
            for q in range(half):
                stage[q, pl.ds(j, rows, stride=some), :] = pot_v[e, z0 + 2 * q]

        reached = [jnp.zeros((some, width), jnp.float32)] * half
        for slot in range(slots):
            for q in range(half):
                code = encode(stage[q, pl.ds(max(slot - 1, 0) * some, some), :] - reached[q])
                enc[z0 + 2 * q + 1, h, slot] = code
                reached[q] = reached[q] + decode(code)

        @pl.when(kind < 2)
        def _():
            @pl.loop(0, half)
            def _(q):
                plane_copy(h, 1 + kind, far0 + q).start()

        @pl.when(kind == 3)
        def _():
            edge_copies(h, facing, lambda copy: copy.start())

        @pl.when(n == 3)
        def _():
            send_near(0)

    @pl.loop(0, readings // 4)
    def _(block):
        for n in range(4):
            m = block * 4 + n
            for c in range(2):
                spots[4 * m + c] = place_s[0, lax.rem(index[4 * m + c], count)]
                spots[4 * m + 2 + c] = place_s[2, index[4 * m + 2 + c]]

    def decode_plane(h, r, slot):
        reached = jnp.zeros((some, width), jnp.float32)
        for k in range(slots):
            reached = reached + decode(cin[r, slot, h, k])
            if k > 0:
                start = (slot * count + h * some) * tall + 8 + r * rows + k - 1
                field[pl.ds(start, some, stride=tall), :] = reached

    row_lane = lax.broadcasted_iota(jnp.int32, (rows, width), 1)

    def gradients(h, b, flat, steep):
        @pl.loop(0, some // GROUP)
        def _(n):
            for e in [h * some + n * GROUP + g for g in range(GROUP)]:

                def at(slot, shift, e=e):
                    return field[pl.ds((slot * count + e) * tall + 8 + b * rows + shift, rows), :]

                for i in steep:
                    own[b, e, 0, i] = ((at(2 + i, 0) - at(i, 0)) * 0.5).astype(jnp.bfloat16)
                for i in flat:
                    here = at(1 + i, 0)
                    right = jnp.where(row_lane < width - 1, pltpu.roll(here, width - 1, 1), 0.0)
                    left = jnp.where(row_lane > 0, pltpu.roll(here, 1, 1), 0.0)
                    own[b, e, 1, i] = ((at(1 + i, 1) - at(1 + i, -1)) * 0.5).astype(jnp.bfloat16)
                    own[b, e, 2, i] = ((right - left) * 0.5).astype(jnp.bfloat16)

    def far_copy(k, step):
        return pltpu.make_async_remote_copy(
            src_ref=box.at[k, step - 1],
            dst_ref=far[k].at[pl.ds((groups - 1 - step) * REQ, REQ)],
            send_sem=far_send.at[k, step],
            recv_sem=far_recv.at[k, step],
            device_id={"elec": lax.rem(group + step, groups)},
            device_id_type=MESH,
        )

    def offer(k, b):
        for step in range(1, groups):
            for which in range(REQ):
                chosen = place_s[0, asked_s[groups - step, 0, which]]
                box[k, step - 1, which] = own[b, chosen]
            far_copy(k, step).start()

    def finish(k, b):
        for step in range(1, groups):
            far_copy(k, step).wait_recv()
        cut = pl.ds(pl.multiple_of(b * rows, rows), rows)
        weight = -(cond_in[:, cut, :].astype(jnp.int32).astype(jnp.float32) * (1.0 / COND_STEPS) + COND_MID)

        @pl.loop(0, readings // 8)
        def _(block):
            for n in range(8):
                m = block * 8 + n
                first, second, third, fourth = (spots[4 * m + c] for c in range(4))
                product = minus(own[b, first], own[b, second]) * minus(far[k][third], far[k][fourth])
                out[m, :, cut, :] = (weight * (product[0] + product[1] + product[2])).astype(jnp.bfloat16)

    def take_near(h):
        @pl.loop(0, half)
        def _(j):
            r = near0 + j

            @pl.when(r == me)
            def _():
                own_planes(h).wait()

            @pl.when(r != me)
            def _():
                plane_wait(h, 1, r)
                plane_wait(h, 2, r)

                @pl.when(me > 0)
                def _():
                    plane_wait(h, 0, r)

                @pl.when(me < slabs - 1)
                def _():
                    plane_wait(h, 3, r)

            @pl.loop(0, 4)
            def _(slot):
                decode_plane(h, r, slot)

    def take_far(h, slot):
        @pl.loop(0, half)
        def _(j):
            r = far0 + j
            plane_wait(h, slot, r)

            @pl.when(downs if slot == 1 else ups)
            def _():
                (forward_down if slot == 1 else forward_up)(h, r).start()

        @pl.loop(0, half)
        def _(j):
            decode_plane(h, far0 + j, slot)

    def take_edges(h):
        @pl.loop(0, half)
        def _(j):
            r = far0 + j

            @pl.when(me < slabs - 1)
            def _():
                plane_wait(h, 3, r)

            decode_plane(h, r, 3)

            @pl.when(me > 0)
            def _():
                plane_wait(h, 0, r)

            decode_plane(h, r, 0)

    inside = upper * (half + 1)
    beyond = (1 - upper) * (half - 1)
    both = (0, 1)

    def each(start, number, act):
        @pl.loop(0, number)
        def _(j):
            act(start + j)

    take_far(0, 1)
    take_near(0)
    each(inside, half - 1, lambda b: gradients(0, b, both, both))
    for k in range(half - 1):
        offer(k, inside + k)
    take_far(0, 2)
    send_near(1)
    take_edges(0)
    each(beyond, half + 1, lambda b: gradients(0, b, both, both))
    for k in range(half + 1):
        offer(half - 1 + k, beyond + k)
    take_far(1, 1)
    take_near(1)
    each(inside, half - 1, lambda b: gradients(1, b, both, both))
    each(beyond, half + 1, lambda b: gradients(1, b, (0,), ()))
    take_far(1, 2)
    for step in range(1, slabs):
        cond_copy(step).wait_recv()
    own_cond.wait()
    for k in range(half - 1):
        finish(k, inside + k)
    each(beyond, half + 1, lambda b: gradients(1, b, (1,), ()))
    take_edges(1)
    each(beyond, half + 1, lambda b: gradients(1, b, (), both))
    for k in range(half + 1):
        finish(half - 1 + k, beyond + k)

    @pl.loop(0, slabs)
    def _(d):
        for h in range(2):

            @pl.when(d != me)
            def _(h=h):
                plane_copy(h, 1, d).wait_send()
                plane_copy(h, 2, d).wait_send()
                edge_copies(h, d, lambda copy: copy.wait_send())

            @pl.when((d // half != upper) & ups)
            def _(h=h):
                forward_up(h, d).wait_send()

            @pl.when((d // half != upper) & downs)
            def _(h=h):
                forward_down(h, d).wait_send()

    for step in range(1, slabs):
        cond_copy(step).wait_send()
    for step in range(1, groups):
        ask_copy(step).wait_send()
    for k in range(slabs):
        for step in range(1, groups):
            far_copy(k, step).wait_send()


def exchange(potentials, conductivity, quadrupoles, slabs, groups):
    count, depth, rows, width = potentials.shape
    readings = quadrupoles.shape[0]
    x_size = rows * slabs
    anywhere = pl.BlockSpec(memory_space=pl.ANY)
    dma = pltpu.SemaphoreType.DMA
    bf16, f32, i16, i32 = jnp.bfloat16, jnp.float32, jnp.int16, jnp.int32
    asks = (groups - 1) * REQ
    return pl.pallas_call(
        functools.partial(exchange_kernel, slabs, groups),
        out_shape=pltpu.VMEM((readings, 2, x_size, width), bf16),
        in_specs=[anywhere, anywhere, pl.BlockSpec(memory_space=pltpu.VMEM), pl.BlockSpec(memory_space=pltpu.SMEM)],
        out_specs=pl.BlockSpec(memory_space=pltpu.VMEM),
        scratch_shapes=[
            pltpu.VMEM((count, depth, rows, width), f32),
            pltpu.VMEM((depth, rows, width), f32),
            pltpu.VMEM((slabs // 2, rows * count // 2, width), f32),
            pltpu.VMEM((depth + 2, 2, rows + 1, count // 2, width), i16),
            pltpu.VMEM((slabs, 4, 2, rows + 1, count // 2, width), i16),
            pltpu.VMEM((4 * count * (x_size + 16), width), f32),
            pltpu.VMEM((depth, rows, width), i16),
            pltpu.VMEM((2, x_size, width), i16),
            pltpu.VMEM((groups, 8, 128), i32),
            pltpu.SMEM((groups, 8, 128), i32),
            pltpu.VMEM((8, 128), i32),
            pltpu.SMEM((8, 128), i32),
            pltpu.VMEM((groups, 8, 128), i32),
            pltpu.SMEM((4 * readings,), i32),
            pltpu.VMEM((slabs, count, 3, 2, rows, width), bf16),
            pltpu.VMEM((slabs, groups - 1, REQ, 3, 2, rows, width), bf16),
        ]
        + [pltpu.VMEM((asks, 3, 2, rows, width), bf16)] * slabs
        + [
            dma((2, 4, slabs)),
            dma((2, 4, slabs)),
            dma((2, 2, slabs)),
            dma((slabs,)),
            dma((slabs,)),
            dma((groups,)),
            dma((groups,)),
            dma((slabs, groups)),
            dma((slabs, groups)),
            dma((PARTS,)),
            dma((6,)),
        ],
        compiler_params=pltpu.CompilerParams(
            collective_id=0, has_side_effects=True, vmem_limit_bytes=50 * 1024 * 1024
        ),
        name="exchange",
    )(potentials, conductivity, quadrupoles, quadrupoles.reshape(-1))


def deliver_kernel(source, target, done):
    share = source.shape[0] // PARTS
    copies = [
        pltpu.make_async_copy(source.at[pl.ds(k * share, share)], target.at[pl.ds(k * share, share)], done.at[k])
        for k in range(PARTS)
    ]
    for copy in copies:
        copy.start()
    for copy in copies:
        copy.wait()


def deliver(rows):
    return pl.pallas_call(
        deliver_kernel,
        out_shape=jax.ShapeDtypeStruct(rows.shape, rows.dtype),
        in_specs=[pl.BlockSpec(memory_space=pl.ANY)],
        out_specs=pl.BlockSpec(memory_space=pl.ANY),
        scratch_shapes=[pltpu.SemaphoreType.DMA((PARTS,))],
        compiler_params=pltpu.CompilerParams(vmem_limit_bytes=1024 * 1024),
        name="deliver",
    )(rows)


def general(potentials, conductivity, quadrupoles):
    shifted = lax.all_to_all(potentials, "slab", split_axis=1, concat_axis=2, tiled=True)
    cond = lax.all_to_all(conductivity[None], "slab", split_axis=1, concat_axis=2, tiled=True)[0]
    slabs = lax.axis_size("slab")
    ends = slabs - 1
    last = shifted.shape[1] - 1
    below = lax.ppermute(shifted[:, last:], "slab", [(i, i + 1) for i in range(ends)])
    above = lax.ppermute(shifted[:, :1], "slab", [(i + 1, i) for i in range(ends)])
    tall = jnp.concatenate([below, shifted, above], axis=1)
    wide = jnp.pad(shifted, ((0, 0), (0, 0), (1, 1), (1, 1)))
    grads = jnp.stack(
        [
            (tall[:, 2:] - tall[:, :-2]) * 0.5,
            (wide[:, :, 2:, 1:-1] - wide[:, :, :-2, 1:-1]) * 0.5,
            (wide[:, :, 1:-1, 2:] - wide[:, :, 1:-1, :-2]) * 0.5,
        ],
        1,
    ).astype(jnp.bfloat16)
    table = lax.all_gather(grads.reshape(grads.shape[0], 3, -1), "elec", axis=0, tiled=True)
    ids = jnp.arange(table.shape[0], dtype=jnp.int32)
    hot = (quadrupoles[:, :, None] == ids).astype(jnp.bfloat16)
    flat = table.reshape(table.shape[0], -1)
    shape = (quadrupoles.shape[0], 3, -1)
    source = jnp.dot(hot[:, 0] - hot[:, 1], flat, preferred_element_type=jnp.float32).reshape(shape)
    probe = jnp.dot(hot[:, 2] - hot[:, 3], flat, preferred_element_type=jnp.float32).reshape(shape)
    rows = -(cond.reshape(-1)[None] * jnp.sum(source * probe, axis=1))
    return rows.astype(jnp.bfloat16).reshape((quadrupoles.shape[0],) + shifted.shape[1:])


def shards(potentials, conductivity, quadrupoles):
    slabs, groups = lax.axis_size("slab"), lax.axis_size("elec")
    count, depth, rows, width = potentials.shape
    fits = rows == 16 and width == 128 and depth == 2 * slabs and slabs % 4 == 0
    if not fits or count % 32 or 2 * (groups - 1) * REQ > count or count * groups != width or quadrupoles.shape[0] % 8:
        return general(potentials, conductivity, quadrupoles)
    return deliver(exchange(potentials, conductivity, quadrupoles, slabs, groups))


def solution(mesh):
    in_specs = (P("elec", None, "slab", None), P(None, "slab", None), P("elec", None))
    out_specs = P("elec", "slab", None, None)
    return jax.shard_map(shards, mesh=mesh, in_specs=in_specs, out_specs=out_specs, check_vma=False)
```
